256 devices in a mesh: bx: 16 (over z, core), by: 16 (over x, y).
Axes of the slice: x: 4, y: 4, z: 8, core: 2. Of those that a mesh axis runs over, the one named last changes fastest.
Arguments:
- right_sides: float32 [256, 256, 8, 256], P('bx', 'by'), may hold values from -6 to 6
- amplitude: float32 [256, 256, 256], P('bx', 'by'), may hold values from 0.5 to 2
- near_list: int32 [256, 256, 9], P('bx', 'by'), may hold values from 0 to 65535, as said below
- far_leaf: int32 [256, 256, 27], P('bx', 'by'), may hold values from 0 to 65535, as said below
- far_one: int32 [128, 128, 27], P('bx', 'by'), may hold values from 0 to 16383, as said below
- far_two: int32 [64, 64, 27], P('bx', 'by'), may hold values from 0 to 4095, as said below
- far_three: int32 [32, 32, 27], P('bx', 'by'), may hold values from 0 to 1023, as said below
- far_four: int32 [16, 16, 27], P('bx', 'by'), may hold values from 0 to 255, as said below
- basis: bfloat16 [256, 64], replicated, may hold values from -0.375 to 0.375
- transfer: bfloat16 [4, 4, 64, 64], replicated, may hold values from -0.5 to 0.5
- coupling: bfloat16 [5, 40, 64, 64], replicated, may hold values from -0.15625 to 0.15625
- near_tiles: bfloat16 [9, 256, 256], replicated, may hold values from -0.125 to 0.125
Outputs:
- product: float32 [256, 256, 8, 256], P('bx', 'by')
The draws below stay inside these ranges and needn't reach their ends.
Inputs may be any that keep to these rules, and one draw needn't show every extreme that they name: Every entry of near_list[i, j, :] names a leaf box, as i2 * 256 + j2, with |i2 - i| <= 1 and |j2 - j| <= 1 (the box itself may be named); entries may repeat, and each entry adds its term. Every entry of far_leaf[i, j, :] names a leaf box, as i2 * 256 + j2, with |i2 - i| <= 3, |j2 - j| <= 3 and max(|i2 - i|, |j2 - j|) >= 2; entries may repeat. Every entry of far_one[i, j, :] names a box of level 1, as i2 * 128 + j2, with |i2 - i| <= 3, |j2 - j| <= 3 and max(|i2 - i|, |j2 - j|) >= 2; entries may repeat. Every entry of far_two[i, j, :] names a box of level 2, as i2 * 64 + j2, with |i2 - i| <= 3, |j2 - j| <= 3 and max(|i2 - i|, |j2 - j|) >= 2; entries may repeat. Every entry of far_three[i, j, :] names a box of level 3, as i2 * 32 + j2, with |i2 - i| <= 3, |j2 - j| <= 3 and max(|i2 - i|, |j2 - j|) >= 2; entries may repeat. Every entry of far_four[i, j, :] names a box of level 4, as i2 * 16 + j2, with |i2 - i| <= 3, |j2 - j| <= 3 and max(|i2 - i|, |j2 - j|) >= 2; entries may repeat.
All inputs are finite; a program needn't handle non-finite values.
Results may differ from the reference program's by a relative error of at most 0.017.
Values may be sent and summed in bfloat16 or wider, within the bound.
A program may use at most 192 MiB of HBM per device.

```python
import math
import jax
import jax.numpy as jnp
from jax import lax

RHS = 8
POINTS = 256
RANK = 64
LEVELS = 5
NEAR = 9
FAR = 27
LEAVES_X = 256
LEAVES_Y = 256


near_table = [(step_x, step_y) for step_x in (-1, 0, 1) for step_y in (-1, 0, 1)]


def parity_table(parity_x, parity_y):
    return [(step_x, step_y) for step_x in range(-2 - parity_x, 4 - parity_x) for step_y in range(-2 - parity_y, 4 - parity_y) if max(abs(step_x), abs(step_y)) >= 2]


def near_offsets(key, slot_count):
    list_shape = (LEAVES_X, LEAVES_Y, slot_count)
    drawn = jax.random.randint(key, list_shape, 0, len(near_table))
    offset_x = jnp.array([pair_entry[0] for pair_entry in near_table], jnp.int32)[drawn]
    offset_y = jnp.array([pair_entry[1] for pair_entry in near_table], jnp.int32)[drawn]
    row_pos = lax.broadcasted_iota(jnp.int32, list_shape, 0)
    col_pos = lax.broadcasted_iota(jnp.int32, list_shape, 1)
    moved_row = row_pos + offset_x
    moved_row = jnp.where((moved_row < 0) | (moved_row >= LEAVES_X), row_pos - offset_x, moved_row)
    moved_col = col_pos + offset_y
    moved_col = jnp.where((moved_col < 0) | (moved_col >= LEAVES_Y), col_pos - offset_y, moved_col)
    return moved_row * LEAVES_Y + moved_col


def settle(position, step, extent):
    moved = position + step
    moved = jnp.where((moved < 0) | (moved >= extent), position - step, moved)
    fallback = jnp.where(position + 2 < extent, position + 2, position - 2)
    return jnp.where((moved < 0) | (moved >= extent), fallback, moved)


def far_offsets(key, height):
    grid_rows = LEAVES_X // 2 ** height
    grid_cols = LEAVES_Y // 2 ** height
    list_shape = (grid_rows, grid_cols, FAR)
    tables = jnp.array([parity_table(parity_x, parity_y) for parity_x in (0, 1) for parity_y in (0, 1)], jnp.int32)
    drawn = jax.random.randint(key, list_shape, 0, 27)
    row_pos = lax.broadcasted_iota(jnp.int32, list_shape, 0)
    col_pos = lax.broadcasted_iota(jnp.int32, list_shape, 1)
    parity = row_pos % 2 * 2 + col_pos % 2
    offset_x = tables[parity, drawn, 0]
    offset_y = tables[parity, drawn, 1]
    moved_row = settle(row_pos, offset_x, grid_rows)
    moved_col = settle(col_pos, offset_y, grid_cols)
    return moved_row * grid_cols + moved_col


def draw_near_list(key, part):
    key = jax.random.fold_in(key, 11)
    return near_offsets(key, NEAR)


def draw_far_leaf(key, part):
    key = jax.random.fold_in(key, 12)
    return far_offsets(key, 0)


def draw_far_one(key, part):
    key = jax.random.fold_in(key, 13)
    return far_offsets(key, 1)


def draw_far_two(key, part):
    key = jax.random.fold_in(key, 14)
    return far_offsets(key, 2)


def draw_far_three(key, part):
    key = jax.random.fold_in(key, 15)
    return far_offsets(key, 3)


def draw_far_four(key, part):
    key = jax.random.fold_in(key, 16)
    return far_offsets(key, 4)


def block_levels(own_key, dims, cuts, smallest, top_value):
    def one(dim, parts):
        steps = jax.random.uniform(jax.random.fold_in(jax.random.fold_in(own_key, 6), dim), (parts,), jnp.float32, smallest / len(cuts), top_value / len(cuts))
        return jnp.repeat(jnp.exp(steps), dims[dim] // parts).reshape((-1,) + (1,) * (len(dims) - dim - 1))

    loudness = one(*cuts[0])
    for cut in cuts[1:]:
        loudness = loudness * one(*cut)
    return loudness


def bell_draw(own_key, shape, scale, reach, pieces=(), kind=jnp.bfloat16):
    loudness = block_levels(own_key, shape, pieces, -0.22, 0.18) if pieces else 1.0
    values = jax.random.normal(own_key, shape, jnp.float32) * scale * loudness
    return jnp.minimum(jnp.maximum(values, -reach), reach).astype(kind)


def setup_inputs(seed: int = 0) -> dict:
    streams_of = jax.random.split(jax.random.key(seed), 13)
    return {
        "right_sides": bell_draw(streams_of[0], (LEAVES_X, LEAVES_Y, RHS, POINTS), 1.0, 6.0, ((0, 16), (1, 16)), jnp.float32),
        "amplitude": jnp.clip(jnp.exp(math.log(2.0) - 1.3862944 * jax.random.uniform(streams_of[1], (LEAVES_X, LEAVES_Y, POINTS), jnp.float32) ** block_levels(streams_of[1], (LEAVES_X, LEAVES_Y, POINTS), ((0, 16), (1, 16)), -0.2, 0.2)), 0.5, 2.0),
        "near_list": draw_near_list(jax.random.fold_in(streams_of[12], 71), 0),
        "far_leaf": draw_far_leaf(jax.random.fold_in(streams_of[12], 71), 0),
        "far_one": draw_far_one(jax.random.fold_in(streams_of[12], 71), 0),
        "far_two": draw_far_two(jax.random.fold_in(streams_of[12], 71), 0),
        "far_three": draw_far_three(jax.random.fold_in(streams_of[12], 71), 0),
        "far_four": draw_far_four(jax.random.fold_in(streams_of[12], 71), 0),
        "basis": bell_draw(streams_of[8], (POINTS, RANK), POINTS ** -0.5, 0.375),
        "transfer": bell_draw(streams_of[9], (LEVELS - 1, 4, RANK, RANK), (2 * RANK) ** -0.5, 0.5),
        "coupling": bell_draw(streams_of[10], (LEVELS, 40, RANK, RANK), (27 * RANK) ** -0.5, 0.15625),
        "near_tiles": bell_draw(streams_of[11], (NEAR, POINTS, POINTS), (9 * POINTS) ** -0.5, 0.125),
    }


near_steps = [(step_x, step_y) for step_x in (-1, 0, 1) for step_y in (-1, 0, 1)]
far_steps = [(step_x, step_y) for step_x in range(-3, 4) for step_y in range(-3, 4) if max(abs(step_x), abs(step_y)) >= 2]


def box_counts(partners, offsets):
    box_cols = partners.shape[1]
    row_pos = lax.broadcasted_iota(jnp.int32, partners.shape, 0)
    col_pos = lax.broadcasted_iota(jnp.int32, partners.shape, 1)
    delta_row = partners // box_cols - row_pos
    delta_col = partners % box_cols - col_pos
    columns = [jnp.sum(((delta_row == step_x) & (delta_col == step_y)).astype(jnp.float32), axis=2) for step_x, step_y in offsets]
    return jnp.stack(columns, axis=2)


def apply_terms(values, counts, matrices, offsets, margin):
    box_rows, box_cols, rhs_count, size_in = values.shape
    size_out = matrices.shape[2]
    block_rows = min(box_rows, 16)
    padded = jnp.pad(values, ((margin, margin), (margin, margin), (0, 0), (0, 0)))
    anchor = jnp.zeros((), jnp.int32)

    def one_block(start):
        summed = jnp.zeros((block_rows, box_cols, rhs_count, size_out), jnp.float32)
        weights = lax.dynamic_slice_in_dim(counts, start, block_rows, 0)
        for number, (step_x, step_y) in enumerate(offsets):
            shifted = lax.dynamic_slice(padded, (start + (margin + step_x), anchor + (margin + step_y), anchor, anchor), (block_rows, box_cols, rhs_count, size_in))
            product = jnp.einsum("abrm,mn->abrn", shifted.astype(jnp.float32), matrices[number].astype(jnp.float32))
            summed = summed + weights[:, :, number, None, None] * product
        return summed

    starts = jnp.arange(0, box_rows, block_rows, dtype=jnp.int32)
    blocks = lax.map(one_block, starts)
    return blocks.reshape(box_rows, box_cols, rhs_count, size_out)


def upward(coefficients, matrices):
    box_rows, box_cols, rhs_count, rank_size = coefficients.shape
    grouped = coefficients.reshape(box_rows // 2, 2, box_cols // 2, 2, rhs_count, rank_size)
    paired = matrices.reshape(2, 2, rank_size, matrices.shape[2])
    return jnp.einsum("aibjrk,ijkm->abrm", grouped.astype(jnp.float32), paired.astype(jnp.float32)).astype(jnp.bfloat16)


def downward(parent, matrices):
    parent_rows, parent_cols, rhs_count, rank_size = parent.shape
    paired = matrices.reshape(2, 2, rank_size, rank_size)
    spread = jnp.einsum("abrm,ijkm->aibjrk", parent.astype(jnp.float32), paired.astype(jnp.float32))
    return spread.reshape(2 * parent_rows, 2 * parent_cols, rhs_count, rank_size)


def reference(right_sides, amplitude, near_list, far_leaf, far_one, far_two, far_three, far_four, basis, transfer, coupling, near_tiles):
    scaled = (amplitude[:, :, None, :] * right_sides).astype(jnp.bfloat16)
    near_counts = box_counts(near_list, near_steps)
    near_field = apply_terms(scaled, near_counts, near_tiles, near_steps, 1)
    levels = [jnp.einsum("abrp,pk->abrk", scaled.astype(jnp.float32), basis.astype(jnp.float32)).astype(jnp.bfloat16)]
    for height in range(transfer.shape[0]):
        levels.append(upward(levels[-1], transfer[height]))
    far_lists = (far_leaf, far_one, far_two, far_three, far_four)
    incoming = None
    for height in range(len(levels) - 1, -1, -1):
        counts = box_counts(far_lists[height], far_steps)
        coupled_terms = apply_terms(levels[height], counts, coupling[height], far_steps, 3)
        if incoming is not None:
            coupled_terms = coupled_terms + downward(incoming, transfer[height])
        incoming = coupled_terms.astype(jnp.bfloat16)
    far_field = jnp.einsum("abrk,pk->abrp", incoming.astype(jnp.float32), basis.astype(jnp.float32))
    return amplitude[:, :, None, :] * (near_field + far_field)
```

```python
import functools

import jax
import jax.numpy as jnp
from jax import lax
from jax.experimental import pallas as pl
from jax.experimental.pallas import tpu as pltpu
from jax.sharding import PartitionSpec as P

MESH = pl.DeviceIdType.MESH
F32 = jnp.float32
BF = jnp.bfloat16

DIRS = [(a, b) for a in (-1, 0, 1) for b in (-1, 0, 1) if (a, b) != (0, 0)]
EDGES = {(-1, 0): 0, (1, 0): 1, (0, -1): 0, (0, 1): 1}
CORNERS = {(-1, -1): 0, (-1, 1): 1, (1, -1): 2, (1, 1): 3}
REACH = (-3, -2, -1, 1, 2, 3)
NEAR = [(p, q) for p in (-1, 0, 1) for q in (-1, 0, 1)]
PAIR_Q = (-3, -1, 1, 2)
PAIRS = [
    (p, m) for p in range(-3, 4) for m in range(4) if abs(p) >= 2 or m in (0, 3)
]
PAIR_COUNT = len(PAIRS)
RUNS = ((0, 0, 5), (6, 5, 7), (14, 12, 19), (34, 31, 7), (42, 38, 2))
GAPS = (5, 13, 33, 41)
SLOTS = 44

NR_ = 8
WI = 22
WJ = 32
NI = 18


def low_half(shape):
    return lax.broadcasted_iota(jnp.int32, shape, len(shape) - 1) < 64


def sel(a, b):
    return jnp.where(low_half(a.shape), a, b)


def swap(v):
    return pltpu.roll(v, 64, 1)


def rounded(v):
    return v.astype(BF).astype(F32)


def dot(a, b):
    return jnp.dot(a, b, preferred_element_type=F32)


def dot_t(a, b):
    return lax.dot_general(a, b, (((1,), (1,)), ((), ())), preferred_element_type=F32)


def kernel(
    size_x, size_y,
    rhs_h, amp_h, nl_h, f0_h, f1_h, f2_h, f3_h, f4_h, basis_h, transfer_h, coupling_h, near_h,
    out_h,
    rhs_v, amp_v, nl_v, f0_v, f1_v, f2_v, f3_v, f4_v, basis_v, transfer_v, coupling_v, near_v,
    s_v, fw, cw, g_v, pairs_v,
    lists_v, nlist_v, counts_v, wn_v, w0_v, w14_v,
    ncs, nks, nr, nc, nk,
    crs, ccs, cks, cr, cc, ck,
    u1_v, c1_v, u2_v, c2_v, q1_v, q2_v, q3_v, u4_v, c4_v,
    d1_v, d2_v, d3_v, d4_v, x1_v, x2_v, x3_v, x4_v, y1_v, y2_v, y3_v, y4_v,
    xn_v, x0_v, acc_v, y0_v,
    load_sem, list_sem, weight_sem, out_sem,
    n_send, n_recv, c_send, c_recv, q1_send, q1_recv, q2_send, q2_recv, t_send, t_recv,
):
    x = lax.axis_index("bx")
    y = lax.axis_index("by")

    def exists(dx, dy):
        ok = True
        tests = []
        if dx < 0:
            tests.append(x >= -dx)
        if dx > 0:
            tests.append(x < size_x - dx)
        if dy < 0:
            tests.append(y >= -dy)
        if dy > 0:
            tests.append(y < size_y - dy)
        ok = tests[0]
        for t in tests[1:]:
            ok = jnp.logical_and(ok, t)
        return ok

    loads = [
        pltpu.make_async_copy(rhs_h.at[:, pl.ds(h * 128, 128)], rhs_v.at[h], load_sem.at[h])
        for h in range(2)
    ] + [
        pltpu.make_async_copy(amp_h.at[:, pl.ds(h * 128, 128)], amp_v.at[h], load_sem.at[2 + h])
        for h in range(2)
    ] + [
        pltpu.make_async_copy(basis_h, basis_v, load_sem.at[4]),
        pltpu.make_async_copy(transfer_h, transfer_v, load_sem.at[5]),
    ]
    list_loads = [
        pltpu.make_async_copy(a, b, list_sem.at[n])
        for n, (a, b) in enumerate(
            ((nl_h, nl_v), (f0_h, f0_v), (f1_h, f1_v), (f2_h, f2_v), (f3_h, f3_v), (f4_h, f4_v))
        )
    ]
    weight_loads = [pltpu.make_async_copy(near_h, near_v, weight_sem.at[0])] + [
        pltpu.make_async_copy(
            coupling_h.at[:, pl.ds(o * 64, n * 64)],
            coupling_v.at[:, pl.ds(s * 64, n * 64)],
            weight_sem.at[1 + k],
        )
        for k, (s, o, n) in enumerate(RUNS)
    ]
    for c in loads + list_loads + weight_loads:
        c.start()

    barrier = pltpu.get_barrier_semaphore()
    partners = DIRS + [(0, b) for b in REACH if abs(b) > 1] + [(a, 0) for a in REACH if abs(a) > 1]
    total = jnp.int32(0)
    for dx, dy in partners:
        ok = exists(dx, dy)

        @pl.when(ok)
        def _():
            pl.semaphore_signal(
                barrier, inc=1, device_id=(x + dx, y + dy), device_id_type=MESH
            )

        total = total + jnp.where(ok, 1, 0).astype(jnp.int32)

    def remote(src, dst, ssem, rsem, dx, dy):
        return pltpu.make_async_remote_copy(
            src_ref=src, dst_ref=dst, send_sem=ssem, recv_sem=rsem,
            device_id=(x + dx, y + dy), device_id_type=MESH,
        )

    def near_copy(d):
        dx, dy = d
        back = DIRS.index((-dx, -dy))
        here = DIRS.index(d)
        if dy == 0:
            src, dst = s_v.at[:, 0 if dx < 0 else 15], nr.at[EDGES[(-dx, 0)]]
        elif dx == 0:
            src, dst = ncs.at[EDGES[d]], nc.at[EDGES[(0, -dy)]]
        else:
            src, dst = nks.at[CORNERS[d]], nk.at[CORNERS[(-dx, -dy)]]
        return remote(src, dst, n_send.at[here], n_recv.at[back], dx, dy)

    def leaf_copy(d):
        dx, dy = d
        back = DIRS.index((-dx, -dy))
        here = DIRS.index(d)
        if dy == 0:
            src, dst = crs.at[EDGES[d]], cr.at[EDGES[(-dx, 0)]]
        elif dx == 0:
            src, dst = ccs.at[EDGES[d]], cc.at[EDGES[(0, -dy)]]
        else:
            src, dst = cks.at[CORNERS[d]], ck.at[CORNERS[(-dx, -dy)]]
        return remote(src, dst, c_send.at[here], c_recv.at[back], dx, dy)

    src1 = {-1: (3, 3), 0: (3, 8), 1: (8, 3)}
    dst1 = {-1: (0, 3), 0: (3, 8), 1: (11, 3)}
    qsrc1 = {-1: (1, 1), 0: (1, 2), 1: (2, 1)}
    qdst1 = {-1: (0, 1), 0: (1, 2), 1: (3, 1)}
    src2 = {-1: (3, 3), 0: (3, 4), 1: (4, 3)}
    dst2 = {-1: (0, 3), 0: (3, 4), 1: (7, 3)}

    def region1(rows, quads):
        return q1_v.at[pl.ds(*rows), pl.ds(*quads)]

    def region2(rows, quad):
        return q2_v.at[pl.ds(*rows), quad]

    def one_copy(d):
        dx, dy = d
        return remote(
            region1(src1[dx], qsrc1[dy]), region1(dst1[-dx], qdst1[-dy]),
            q1_send.at[DIRS.index(d)], q1_recv.at[DIRS.index((-dx, -dy))], dx, dy,
        )

    def two_copy(d):
        dx, dy = d
        return remote(
            region2(src2[dx], 1), region2(dst2[-dx], 1 - dy),
            q2_send.at[DIRS.index(d)], q2_recv.at[DIRS.index((-dx, -dy))], dx, dy,
        )

    def along_copy(b):
        k = REACH.index(b)
        return remote(
            q3_v.at[3, 3], q3_v.at[3, 3 - b], t_send.at[k], t_recv.at[REACH.index(-b)], 0, b
        )

    def across_copy(a):
        k = REACH.index(a)
        return remote(
            q3_v.at[3], q3_v.at[3 - a], t_send.at[6 + k], t_recv.at[6 + REACH.index(-a)], a, 0
        )

    def start(copy, d):
        @pl.when(exists(*d))
        def _():
            copy.start()

    def arrived(copy, d):
        @pl.when(exists(*d))
        def _():
            copy.wait_recv()

    def sent(copy, d):
        @pl.when(exists(*d))
        def _():
            copy.wait_send()

    def blank(ref, d):
        @pl.when(jnp.logical_not(exists(*d)))
        def _():
            ref[...] = jnp.zeros(ref.shape, ref.dtype)

    for d in DIRS:
        dx, dy = d
        if dy == 0:
            blank(nr.at[EDGES[d]], d)
            blank(cr.at[EDGES[d]], d)
        elif dx == 0:
            blank(nc.at[EDGES[d]], d)
            blank(cc.at[EDGES[d]], d)
        else:
            blank(nk.at[CORNERS[d]], d)
            blank(ck.at[CORNERS[d]], d)
        blank(region1(dst1[dx], qdst1[dy]), d)
        blank(region2(dst2[dx], 1 + dy), d)
    for b in REACH:
        blank(q3_v.at[3, 3 + b], (0, b))
    for a in REACH:
        blank(q3_v.at[3 + a], (a, 0))
    for level in range(5):
        for s in GAPS:
            coupling_v[level, pl.ds(s * 64, 64)] = jnp.zeros((64, 64), BF)

    for c in loads[:4]:
        c.wait()

    def scale_row(i, carry):
        for h in range(2):
            amp_low = amp_v[h, pl.ds(i * 16, 8), :]
            amp_high = amp_v[h, pl.ds(i * 16 + 8, 8), :]
            for r in range(NR_):
                low = rhs_v[h, pl.ds(i * 128 + r, 8, stride=8), :] * amp_low
                high = rhs_v[h, pl.ds(i * 128 + 64 + r, 8, stride=8), :] * amp_high
                value = jnp.concatenate([low, high], axis=0).astype(BF)
                s_v[r, i, :, pl.ds(h * 128, 128)] = value
                fw[h, pl.ds(pl.multiple_of((r * NI + i + 1) * WJ + 8, 8), 16), :] = value.astype(F32)
        return carry

    lax.fori_loop(0, 16, scale_row, 0)

    def near_pack(r, carry):
        for k, j in ((0, 0), (1, 15)):
            for h in range(2):
                base = (r * NI + 1) * WJ + 8 + j
                rows = [fw[h, pl.ds(base + 8 * WJ * t, 8, stride=WJ), :] for t in range(2)]
                ncs[k, r, :, pl.ds(h * 128, 128)] = jnp.concatenate(rows, axis=0).astype(BF)
        return carry

    lax.fori_loop(0, NR_, near_pack, 0)
    for (dx, dy), k in CORNERS.items():
        i, j = (0 if dx < 0 else 15), (0 if dy < 0 else 15)
        for h in range(2):
            nks[k, :, pl.ds(h * 128, 128)] = fw[
                h, pl.ds((i + 1) * WJ + 8 + j, 8, stride=NI * WJ), :
            ]
    pl.semaphore_wait(barrier, total)
    for d in DIRS:
        start(near_copy(d), d)

    for c in loads[4:]:
        c.wait()
    basis = basis_v[...]
    basis_twice = jnp.concatenate([basis, basis], axis=0)

    def leaf_level(r, carry):
        value = rounded(dot_t(s_v[r].reshape(256, 256), basis_twice))
        for i in range(16):
            cw[pl.ds(pl.multiple_of((r * WI + i + 3) * WJ + 8, 8), 16), :] = value[i * 16 : (i + 1) * 16]
        return carry

    lax.fori_loop(0, NR_, leaf_level, 0)

    def leaf_pack(r, carry):
        for k, first in ((0, 0), (1, 13)):
            for t in range(3):
                rows = [
                    cw[pl.ds(((r + u) * WI + 3 + first + t) * WJ + 8, 16), :] for u in (0, 4)
                ]
                crs[k, r, t] = sel(rows[0], rows[1]).astype(BF)
                cols = [
                    jnp.concatenate(
                        [
                            cw[
                                pl.ds(((r + u) * WI + 3 + 8 * v) * WJ + 8 + first + t, 8, stride=WJ),
                                :,
                            ]
                            for v in range(2)
                        ],
                        axis=0,
                    )
                    for u in (0, 4)
                ]
                ccs[k, r, t] = sel(cols[0], cols[1]).astype(BF)
        return carry

    lax.fori_loop(0, 4, leaf_pack, 0)

    def leaf_box(i, j):
        return cw[pl.ds(i * WJ + j, 8, stride=WI * WJ), :]

    for (dx, dy), k in CORNERS.items():
        first_i, first_j = (3 if dx < 0 else 16), (8 if dy < 0 else 21)
        for t in range(3):
            box = [leaf_box(first_i + t, first_j + u) for u in range(3)]
            cks[k, t] = jnp.concatenate([sel(box[0], box[2]), box[1]], axis=0).astype(BF)
    for d in DIRS:
        start(leaf_copy(d), d)

    def twice(level):
        t = transfer_v[level]
        return jnp.concatenate([t, t], axis=1)

    def gather_one(i, carry):
        for j in range(0, 8, 2):
            tiles = []
            for u in range(2):
                box = [
                    leaf_box(3 + 2 * i + a, 8 + 2 * (j + u) + b) for a in range(2) for b in range(2)
                ]
                tiles.append(
                    jnp.concatenate([sel(box[0], box[1]), sel(box[2], box[3])], axis=1)
                )
            u1_v[pl.ds(pl.multiple_of(i * 64 + j * 8, 16), 16), :] = jnp.concatenate(tiles, axis=0).astype(BF)
        return carry

    lax.fori_loop(0, 8, gather_one, 0)
    c1_v[...] = rounded(dot(u1_v[...], twice(0))).reshape(64, 8, 128)

    def quad_one(i, carry):
        for g in range(2):
            box = [c1_v[i * 8 + 4 * g + u] for u in range(4)]
            q1_v[3 + i, 1 + g] = jnp.concatenate(
                [sel(box[0], box[2]), sel(box[1], box[3])], axis=0
            ).astype(BF)
        return carry

    lax.fori_loop(0, 8, quad_one, 0)
    for d in DIRS:
        start(one_copy(d), d)

    def parents(children, n, i, j):
        box = [children[(2 * i + a) * 2 * n + 2 * j + b] for a in range(2) for b in range(2)]
        return jnp.concatenate([sel(box[0], box[1]), sel(box[2], box[3])], axis=1)

    def quad(box):
        return jnp.concatenate([sel(box[0], box[2]), sel(box[1], box[3])], axis=0).astype(BF)

    for i in range(4):
        for j in range(0, 4, 2):
            u2_v[pl.ds((i * 4 + j) * 8, 16), :] = jnp.concatenate(
                [parents(c1_v, 4, i, j + u) for u in range(2)], axis=0
            ).astype(BF)
    c2_v[...] = rounded(dot(u2_v[...], twice(1))).reshape(16, 8, 128)
    for i in range(4):
        q2_v[3 + i, 1] = quad([c2_v[i * 4 + u] for u in range(4)])
    for d in DIRS:
        start(two_copy(d), d)
    up = jnp.concatenate(
        [parents(c2_v, 2, i, j) for i in range(2) for j in range(2)], axis=0
    ).astype(BF)
    c3 = rounded(dot(up, twice(2)))
    q3_v[3, 3] = quad([c3[u * 8 : (u + 1) * 8] for u in range(4)])
    for b in REACH:
        start(along_copy(b), (0, b))

    for c in list_loads:
        c.wait()
    lists_v[...] = jnp.full(lists_v.shape, -1000000.0, F32)
    lists_v[pl.ds(0, 256), pl.ds(0, 27)] = f0_v[...].astype(F32)
    lists_v[pl.ds(256, 64), pl.ds(0, 27)] = f1_v[...].astype(F32)
    for i in range(4):
        lists_v[pl.ds(320 + 4 * i, 4), pl.ds(0, 27)] = f2_v[i].astype(F32)
    for i in range(2):
        lists_v[pl.ds(336 + 2 * i, 2), pl.ds(0, 27)] = f3_v[i].astype(F32)
    lists_v[pl.ds(340, 1), pl.ds(0, 27)] = f4_v[0].astype(F32)
    nlist_v[...] = jnp.full(nlist_v.shape, -1000000.0, F32)
    for s in range(9):
        nlist_v[pl.ds(16 * s, 16), pl.ds(0, 16)] = nl_v[s].astype(F32)

    far_t = jnp.concatenate(
        [jnp.transpose(lists_v[pl.ds(128 * t, 128), :])[0:32] for t in range(3)], axis=1
    )
    lane = lax.broadcasted_iota(jnp.int32, (1, 384), 1)
    level_of = [(0, 0, 16, 4), (256, 1, 8, 3), (320, 2, 4, 2), (336, 3, 2, 1), (340, 4, 1, 0)]
    base = jnp.zeros((1, 384), jnp.int32)
    pitch = jnp.zeros((1, 384), jnp.int32)
    for first, level, n, shift in level_of:
        local = lane - first
        cols = n * size_y
        mine = (x * n + lax.shift_right_arithmetic(local, shift)) * cols + y * n + (local & (n - 1))
        base = jnp.where(local >= 0, mine, base)
        pitch = jnp.where(local >= 0, cols, pitch)
    far_t = far_t - base.astype(F32)
    pitch = pitch.astype(F32)
    counts_v[...] = jnp.zeros(counts_v.shape, F32)

    def far_count(p, carry):
        row = (p - 3).astype(F32) * pitch
        for k, q in enumerate((-3, -2, -1, 0, 1, None, 2, 3)):
            if q is not None:
                hits = jnp.where(far_t == row + float(q), 1.0, 0.0)
                counts_v[pl.ds(p * 8 + k, 1), :] = jnp.sum(hits, axis=0, keepdims=True)
        return carry

    lax.fori_loop(0, 7, far_count, 0)
    near_t = []
    group = lax.broadcasted_iota(jnp.int32, (16, 128), 1) // 16
    for half in range(2):
        got = jnp.full((16, 128), -1000000.0, F32)
        for k in range(8):
            piece = nlist_v[pl.ds(half * 8 + k, 16, stride=16), :]
            if k:
                piece = pltpu.roll(piece, 16 * k, 1)
            got = jnp.where(group == k, piece, got)
        near_t.append(got)
    near_t = jnp.concatenate(near_t, axis=1) - base[:, 0:256].astype(F32)
    for o, (p, q) in enumerate(NEAR):
        hits = jnp.where(near_t == float(p) * float(16 * size_y) + float(q), 1.0, 0.0)
        counts_v[pl.ds(64 + o, 1), pl.ds(0, 256)] = jnp.sum(hits, axis=0, keepdims=True)
    counts = jnp.concatenate(
        [jnp.transpose(counts_v[:, pl.ds(128 * t, 128)]) for t in range(3)], axis=0
    ).astype(BF)
    source = lax.broadcasted_iota(jnp.int32, (128, 128), 0)
    half_of = lax.broadcasted_iota(jnp.int32, (128, 128), 1) // 64
    for t, (p, m) in enumerate(PAIRS):
        k = (p + 3) * 8 + 2 * m
        spread = jnp.where(source == k + half_of, 1.0, 0.0).astype(BF)
        weights = dot(counts, spread)
        w0_v[:, pl.ds(128 * t, 128)] = weights[0:256].astype(BF)
        w14_v[t] = weights[256:384]
    for o in range(9):
        spread = jnp.where(source == 64 + o, 1.0, 0.0).astype(BF)
        wn_v[:, pl.ds(128 * o, 128)] = dot(counts[0:256], spread).astype(BF)

    for b in REACH:
        arrived(along_copy(-b), (0, b))
    for a in REACH:
        start(across_copy(a), (a, 0))

    for d in DIRS:
        arrived(near_copy((-d[0], -d[1])), d)

    def near_unpack(r, carry):
        for k, ii, jj in ((0, 0, 7), (1, 17, 24)):
            for h in range(2):
                fw[h, pl.ds(pl.multiple_of((r * NI + ii) * WJ + 8, 8), 16), :] = nr[
                    k, r, :, pl.ds(h * 128, 128)
                ].astype(F32)
                column = nc[k, r, :, pl.ds(h * 128, 128)].astype(F32)
                for t in range(2):
                    fw[h, pl.ds((r * NI + 1 + 8 * t) * WJ + jj, 8, stride=WJ), :] = column[
                        8 * t : 8 * t + 8
                    ]
        return carry

    lax.fori_loop(0, NR_, near_unpack, 0)
    for (dx, dy), k in CORNERS.items():
        ii, jj = (0 if dx < 0 else 17), (7 if dy < 0 else 24)
        for h in range(2):
            fw[h, pl.ds(ii * WJ + jj, 8, stride=NI * WJ), :] = nk[k, :, pl.ds(h * 128, 128)]
    for c in weight_loads:
        c.wait()

    def near_block(block, carry):
        for u in range(2):
            i = block * 2 + u
            for o, (p, q) in enumerate(NEAR):
                w = wn_v[pl.ds(pl.multiple_of(i * 16, 16), 16), pl.ds(128 * o, 128)]
                for r in range(NR_):
                    for h in range(2):
                        first = (r * NI + i + 1 + p) * WJ + 8 + q
                        if q == 0:
                            first = pl.multiple_of(first, 8)
                        value = fw[h, pl.ds(first, 16), :].astype(BF) * w
                        xn_v[pl.ds(u * 128 + r * 16, 16), pl.ds(o * 256 + h * 128, 128)] = value
        acc_v[pl.ds(pl.multiple_of(block * 256, 256), 256), :] = dot(xn_v[...], near_v[...])
        return carry

    lax.fori_loop(0, 8, near_block, 0)

    for d in DIRS:
        arrived(leaf_copy((-d[0], -d[1])), d)

    def leaf_unpack(r, carry):
        for k in range(2):
            for t in range(3):
                row = cr[k, r, t].astype(F32)
                other = swap(row)
                column = cc[k, r, t].astype(F32)
                across = swap(column)
                ii = t + (0, 19)[k]
                jj = t + (5, 24)[k]
                for u, value, col in (
                    (0, sel(row, other), sel(column, across)),
                    (4, sel(other, row), sel(across, column)),
                ):
                    cw[pl.ds(pl.multiple_of(((r + u) * WI + ii) * WJ + 8, 8), 16), :] = value
                    for v in range(2):
                        cw[pl.ds(((r + u) * WI + 3 + 8 * v) * WJ + jj, 8, stride=WJ), :] = col[
                            8 * v : 8 * v + 8
                        ]
        return carry

    lax.fori_loop(0, 4, leaf_unpack, 0)
    for (dx, dy), k in CORNERS.items():
        for t in range(3):
            value = ck[k, t].astype(F32)
            other = swap(value)
            ii = t + (0 if dx < 0 else 19)
            for u in range(3):
                jj = u + (5 if dy < 0 else 24)
                rows = slice(8, 16) if u == 1 else slice(0, 8)
                box = sel(other, value) if u == 2 else sel(value, other)
                cw[pl.ds(ii * WJ + jj, 8, stride=WI * WJ), :] = box[rows]

    def pair_row(ri, carry):
        base = ri * WJ
        for m, q in enumerate(PAIR_Q):
            a = cw[pl.ds(base + 8 + q, 16), :]
            b = cw[pl.ds(base + 9 + q, 16), :]
            pairs_v[m, ri] = sel(a, b).astype(BF)
        return carry

    lax.fori_loop(0, NR_ * WI, pair_row, 0)

    def leaf_block(block, carry):
        for u in range(2):
            i = block * 2 + u
            for t, (p, m) in enumerate(PAIRS):
                w = w0_v[pl.ds(pl.multiple_of(i * 16, 16), 16), pl.ds(128 * t, 128)]
                for r in range(NR_):
                    x0_v[pl.ds(u * 128 + r * 16, 16), pl.ds(128 * t, 128)] = (
                        pairs_v[m, r * WI + i + 3 + p] * w
                    )
        y0_v[pl.ds(pl.multiple_of(block * 256, 256), 256), :] = dot(x0_v[...], coupling_v[0])
        return carry

    lax.fori_loop(0, 8, leaf_block, 0)

    for d in DIRS:
        arrived(one_copy((-d[0], -d[1])), d)
        arrived(two_copy((-d[0], -d[1])), d)
    for a in REACH:
        arrived(across_copy(-a), (a, 0))

    def quad_parts(value):
        value = value.astype(F32)
        low, high = value[0:8], value[8:16]
        return low, high, swap(low), swap(high)

    def quad_row(dst, row, quads, first, last):
        parts = [quad_parts(v) for v in quads]
        for g, (lo, hi, lo_s, hi_s) in enumerate(parts):
            values = [sel(lo, hi_s), sel(hi, lo), sel(lo_s, hi)]
            if g + 1 < len(parts):
                values.append(sel(hi_s, parts[g + 1][2]))
            for u, value in enumerate(values):
                col = 4 * g + u - 1
                if first <= col < last:
                    dst[row, col] = value

    def rows_one(i, carry):
        quad_row(d1_v, i, [q1_v[i, g] for g in range(4)], 0, 13)
        return carry

    lax.fori_loop(0, 14, rows_one, 0)

    def rows_two(i, carry):
        quad_row(d2_v, i, [q2_v[i, g] for g in range(3)], 0, 9)
        return carry

    lax.fori_loop(0, 10, rows_two, 0)

    def rows_three(dev, carry):
        parts = [quad_parts(q3_v[dev, g]) for g in range(7)]
        for a in range(2):
            @pl.when(jnp.logical_and(2 * dev + a >= 3, 2 * dev + a <= 10))
            def _():
                for col in range(7):
                    g, b = (col + 3) // 2, (col + 3) % 2
                    lo, hi, lo_s, hi_s = parts[g]
                    lo_n, _, lo_sn, _ = parts[g + 1]
                    if b == 0:
                        value = sel(lo, hi_s) if a == 0 else sel(lo_s, hi)
                    else:
                        value = sel(hi, lo_sn) if a == 0 else sel(hi_s, lo_n)
                    d3_v[2 * dev + a - 3, col] = value
        for g in range(7):
            lo, hi, lo_s, hi_s = parts[g]
            u4_v[dev, pl.ds(g * 8, 8), :] = jnp.concatenate([sel(lo, hi_s), sel(lo_s, hi)], axis=1)
        return carry

    lax.fori_loop(0, 7, rows_three, 0)
    c4_v[...] = rounded(dot(u4_v[...].reshape(392, 256).astype(BF), twice(3))).reshape(7, 56, 128)
    for i in range(7):
        for j in range(6):
            d4_v[i, j] = sel(c4_v[i, pl.ds(8 * j, 8), :], c4_v[i, pl.ds(8 * j + 8, 8), :])

    def fill(dst, window, n, first):
        def two_boxes(h, carry):
            tiles = []
            places = []
            for u in range(2):
                b = h * 2 + u if n > 1 else 0
                places.append((b // n, b % n, first + b))
            for t, (p, m) in enumerate(PAIRS):
                tiles = []
                for i, j, b in places:
                    w = w14_v[t, pl.ds(b, 1), :]
                    tiles.append(window[i + 3 + p, j + 3 + PAIR_Q[m]] * jnp.broadcast_to(w, (8, 128)))
                dst[pl.ds(pl.multiple_of(h * 16, 16), 16), pl.ds(128 * t, 128)] = jnp.concatenate(tiles, axis=0).astype(BF)
            return carry

        lax.fori_loop(0, max(1, n * n // 2), two_boxes, 0)

    fill(x4_v, d4_v, 1, 84)
    fill(x3_v, d3_v, 2, 80)
    fill(x2_v, d2_v, 4, 64)
    fill(x1_v, d1_v, 8, 0)
    down = dot(x4_v[...], coupling_v[4])[0:8].astype(BF)
    for level, n, xs, ys in ((3, 2, x3_v, y3_v), (2, 4, x2_v, y2_v), (1, 8, x1_v, y1_v)):
        ys[...] = dot(xs[...], coupling_v[level])
        for a in range(2):
            for b in range(2):
                spread = dot_t(down, transfer_v[level, pl.ds((2 * a + b) * 64, 64), :])
                for i in range(n // 2):
                    for j in range(n // 2):
                        at = ((2 * i + a) * n + 2 * j + b) * 8
                        part = (i * (n // 2) + j) * 8
                        ys[pl.ds(at, 8), :] += spread[part : part + 8]
        down = ys[...].astype(BF)
    for a in range(2):
        for b in range(2):
            t = transfer_v[0, pl.ds((2 * a + b) * 64, 64), :]
            spread = dot_t(down, jnp.concatenate([t, t], axis=0))
            for i in range(8):
                for j in range(8):
                    at = (2 * i + a) * 128 + 2 * j + b
                    part = (i * 8 + j) * 8
                    g_v[pl.ds(at, 8, stride=16), :] = spread[part : part + 8]

    def finish(block, carry):
        rows = pl.ds(pl.multiple_of(block * 256, 256), 256)
        d0 = (y0_v[rows, :] + g_v[rows, pl.ds(0, 64)]).astype(BF)
        value = acc_v[rows, :] + dot(d0, basis)
        for u in range(2):
            i = block * 2 + u
            for r in range(NR_):
                for v in range(2):
                    for h in range(2):
                        at = u * 128 + r * 16 + 8 * v
                        rhs_v[h, pl.ds(i * 128 + v * 64 + r, 8, stride=8), :] = value[
                            at : at + 8, h * 128 : (h + 1) * 128
                        ]
        return carry

    lax.fori_loop(0, 8, finish, 0)
    outs = [
        pltpu.make_async_copy(rhs_v.at[h], out_h.at[:, pl.ds(h * 128, 128)], out_sem.at[h])
        for h in range(2)
    ]
    for c in outs:
        c.start()
    for d in DIRS:
        for copy in (near_copy, leaf_copy, one_copy, two_copy):
            sent(copy(d), d)
    for b in REACH:
        sent(along_copy(b), (0, b))
    for a in REACH:
        sent(across_copy(a), (a, 0))
    for c in outs:
        c.wait()


def body(
    right_sides, amplitude, near_list, far_leaf, far_one, far_two, far_three, far_four,
    basis, transfer, coupling, near_tiles,
):
    size_x, size_y = lax.axis_size("bx"), lax.axis_size("by")
    dma = pltpu.SemaphoreType.DMA
    vmem = pltpu.VMEM
    i32 = jnp.int32
    operands = (
        right_sides.reshape(2048, 256), amplitude.reshape(256, 256),
        jnp.transpose(near_list, (2, 0, 1)), far_leaf.reshape(256, 27), far_one.reshape(64, 27),
        far_two, far_three, far_four, basis.T, transfer.reshape(4, 256, 64),
        coupling.reshape(5, 2560, 64), near_tiles.reshape(2304, 256),
    )
    scratch = [
        vmem((2, 2048, 128), F32), vmem((2, 256, 128), F32), vmem((9, 16, 16), i32),
        vmem((256, 27), i32), vmem((64, 27), i32), vmem((4, 4, 27), i32), vmem((2, 2, 27), i32),
        vmem((1, 1, 27), i32), vmem((64, 256), BF), vmem((4, 256, 64), BF),
        vmem((5, SLOTS * 64, 64), BF), vmem((2304, 256), BF),
        vmem((8, 16, 16, 256), BF), vmem((2, NR_ * NI * WJ, 128), F32),
        vmem((NR_ * WI * WJ, 128), F32), vmem((2048, 128), F32), vmem((4, NR_ * WI, 16, 128), BF),
        vmem((384, 128), F32), vmem((256, 128), F32), vmem((128, 384), F32),
        vmem((256, 9 * 128), BF), vmem((256, PAIR_COUNT * 128), BF), vmem((PAIR_COUNT, 128, 128), F32),
        vmem((2, 8, 16, 256), BF), vmem((4, 8, 256), F32),
        vmem((2, 8, 16, 256), BF), vmem((2, 8, 16, 256), BF), vmem((4, 8, 256), F32),
        vmem((2, 4, 3, 16, 128), BF), vmem((2, 4, 3, 16, 128), BF), vmem((4, 3, 16, 128), BF),
        vmem((2, 4, 3, 16, 128), BF), vmem((2, 4, 3, 16, 128), BF), vmem((4, 3, 16, 128), BF),
        vmem((512, 256), BF), vmem((64, 8, 128), F32), vmem((128, 256), BF), vmem((16, 8, 128), F32),
        vmem((14, 4, 16, 128), BF), vmem((10, 3, 16, 128), BF), vmem((7, 7, 16, 128), BF),
        vmem((7, 56, 256), F32), vmem((7, 56, 128), F32),
        vmem((14, 13, 8, 128), F32), vmem((10, 9, 8, 128), F32), vmem((8, 7, 8, 128), F32),
        vmem((7, 6, 8, 128), F32),
        vmem((512, SLOTS * 64), BF), vmem((128, SLOTS * 64), BF), vmem((32, SLOTS * 64), BF),
        vmem((16, SLOTS * 64), BF),
        vmem((512, 64), F32), vmem((128, 64), F32), vmem((32, 64), F32), vmem((16, 64), F32),
        vmem((256, 2304), BF), vmem((256, SLOTS * 64), BF), vmem((2048, 256), F32),
        vmem((2048, 64), F32),
        dma((6,)), dma((6,)), dma((6,)), dma((2,)),
        dma((8,)), dma((8,)), dma((8,)), dma((8,)), dma((8,)), dma((8,)), dma((8,)), dma((8,)),
        dma((12,)), dma((12,)),
    ]
    total = pl.pallas_call(
        functools.partial(kernel, size_x, size_y),
        out_shape=jax.ShapeDtypeStruct((2048, 256), F32),
        in_specs=[pl.BlockSpec(memory_space=pl.ANY)] * len(operands),
        out_specs=pl.BlockSpec(memory_space=pl.ANY),
        scratch_shapes=scratch,
        compiler_params=pltpu.CompilerParams(
            collective_id=0, has_side_effects=True, vmem_limit_bytes=56 * 1024 * 1024
        ),
        cost_estimate=pl.CostEstimate(
            flops=12_000_000_000, bytes_accessed=10_000_000, transcendentals=0
        ),
    )(*operands)
    return amplitude[:, :, None, :] * total.reshape(right_sides.shape)


def solution(mesh):
    split3 = P("bx", "by", None)
    placed = (P("bx", "by", None, None),) + (split3,) * 7 + (P(),) * 4
    return jax.shard_map(
        body, mesh=mesh, in_specs=placed, out_specs=P("bx", "by", None, None), check_vma=False
    )
```

```python
import functools

import jax
import jax.numpy as jnp
from jax import lax
from jax.experimental import pallas as pl
from jax.experimental.pallas import tpu as pltpu
from jax.sharding import PartitionSpec as P

MESH = pl.DeviceIdType.MESH
F32 = jnp.float32
BF = jnp.bfloat16

DIRS = [(a, b) for a in (-1, 0, 1) for b in (-1, 0, 1) if (a, b) != (0, 0)]
EDGES = {(-1, 0): 0, (1, 0): 1, (0, -1): 0, (0, 1): 1}
CORNERS = {(-1, -1): 0, (-1, 1): 1, (1, -1): 2, (1, 1): 3}
REACH = (-3, -2, -1, 1, 2, 3)
NEAR = [(p, q) for p in (-1, 0, 1) for q in (-1, 0, 1)]
PAIR_Q = (-3, -1, 1, 2)
PAIRS = [
    (p, m) for p in range(-3, 4) for m in range(4) if abs(p) >= 2 or m in (0, 3)
]
PAIR_COUNT = len(PAIRS)
RUNS = ((0, 0, 5), (6, 5, 7), (14, 12, 19), (34, 31, 7), (42, 38, 2))
GAPS = (5, 13, 33, 41)
SLOTS = 44
NEAR_ROWS = 4
LEAF_ROWS = 4

NR_ = 8
WI = 22
WJ = 32
NI = 18


def low_half(shape):
    return lax.broadcasted_iota(jnp.int32, shape, len(shape) - 1) < 64


def sel(a, b):
    return jnp.where(low_half(a.shape), a, b)


def aligned(v, n):
    return v if isinstance(v, int) else pl.multiple_of(v, n)


def swap(v):
    return pltpu.roll(v, 64, 1)


def rounded(v):
    return v.astype(BF).astype(F32)


def dot(a, b):
    return jnp.dot(a, b, preferred_element_type=F32)


def dot_t(a, b):
    return lax.dot_general(a, b, (((1,), (1,)), ((), ())), preferred_element_type=F32)


def kernel(
    size_x, size_y,
    rhs_h, amp_h, nl_h, f0_h, f1_h, f2_h, f3_h, f4_h, basis_h, transfer_h, coupling_h, near_h,
    near_out_h, leaf_out_h,
    rhs_v, amp_v, nl_v, f0_v, f1_v, f2_v, f3_v, f4_v, basis_v, transfer_v, coupling_v, near_v,
    s_v, fw, cw, g_v, pairs_v,
    lists_v, nlist_v, counts_v, wn_v, w0_v, w14_v,
    ncs, nks, nr, nc, nk,
    crs, ccs, cks, cr, cc, ck,
    u1_v, c1_v, u2_v, c2_v, q1_v, q2_v, q3_v, u4_v, c4_v,
    d1_v, d2_v, d3_v, d4_v, x1_v, x2_v, x3_v, x4_v, y1_v, y2_v, y3_v, y4_v,
    acc_v, y0_v, d0_v,
    load_sem, list_sem, weight_sem, out_sem,
    n_send, n_recv, c_send, c_recv, q1_send, q1_recv, q2_send, q2_recv, t_send, t_recv,
):
    x = lax.axis_index("bx")
    y = lax.axis_index("by")

    def exists(dx, dy):
        ok = True
        tests = []
        if dx < 0:
            tests.append(x >= -dx)
        if dx > 0:
            tests.append(x < size_x - dx)
        if dy < 0:
            tests.append(y >= -dy)
        if dy > 0:
            tests.append(y < size_y - dy)
        ok = tests[0]
        for t in tests[1:]:
            ok = jnp.logical_and(ok, t)
        return ok

    loads = [
        pltpu.make_async_copy(
            rhs_h.at[pl.ds(c * 512, 512), pl.ds(h * 128, 128)],
            rhs_v.at[h, pl.ds(c * 512, 512)],
            load_sem.at[2 * c + h],
        )
        for c in range(4)
        for h in range(2)
    ]
    small_loads = [
        pltpu.make_async_copy(amp_h.at[:, pl.ds(h * 128, 128)], amp_v.at[h], load_sem.at[8 + h])
        for h in range(2)
    ] + [
        pltpu.make_async_copy(basis_h, basis_v, load_sem.at[10]),
        pltpu.make_async_copy(transfer_h, transfer_v, load_sem.at[11]),
    ]
    list_loads = [
        pltpu.make_async_copy(a, b, list_sem.at[n])
        for n, (a, b) in enumerate(
            ((nl_h, nl_v), (f0_h, f0_v), (f1_h, f1_v), (f2_h, f2_v), (f3_h, f3_v), (f4_h, f4_v))
        )
    ]
    weight_loads = [pltpu.make_async_copy(near_h, near_v, weight_sem.at[0])] + [
        pltpu.make_async_copy(
            coupling_h.at[:, pl.ds(o * 64, n * 64)],
            coupling_v.at[:, pl.ds(s * 64, n * 64)],
            weight_sem.at[1 + k],
        )
        for k, (s, o, n) in enumerate(RUNS)
    ]
    for c in small_loads[:2] + loads + small_loads[2:] + list_loads:
        c.start()

    barrier = pltpu.get_barrier_semaphore()
    partners = DIRS + [(0, b) for b in REACH if abs(b) > 1] + [(a, 0) for a in REACH if abs(a) > 1]
    total = jnp.int32(0)
    for dx, dy in partners:
        ok = exists(dx, dy)

        @pl.when(ok)
        def _():
            pl.semaphore_signal(
                barrier, inc=1, device_id=(x + dx, y + dy), device_id_type=MESH
            )

        total = total + jnp.where(ok, 1, 0).astype(jnp.int32)

    def remote(src, dst, ssem, rsem, dx, dy):
        return pltpu.make_async_remote_copy(
            src_ref=src, dst_ref=dst, send_sem=ssem, recv_sem=rsem,
            device_id=(x + dx, y + dy), device_id_type=MESH,
        )

    def near_copy(d):
        dx, dy = d
        back = DIRS.index((-dx, -dy))
        here = DIRS.index(d)
        if dy == 0:
            src, dst = s_v.at[:, 0 if dx < 0 else 15], nr.at[EDGES[(-dx, 0)]]
        elif dx == 0:
            src, dst = ncs.at[EDGES[d]], nc.at[EDGES[(0, -dy)]]
        else:
            src, dst = nks.at[CORNERS[d]], nk.at[CORNERS[(-dx, -dy)]]
        return remote(src, dst, n_send.at[here], n_recv.at[back], dx, dy)

    def leaf_copy(d):
        dx, dy = d
        back = DIRS.index((-dx, -dy))
        here = DIRS.index(d)
        if dy == 0:
            src, dst = crs.at[EDGES[d]], cr.at[EDGES[(-dx, 0)]]
        elif dx == 0:
            src, dst = ccs.at[EDGES[d]], cc.at[EDGES[(0, -dy)]]
        else:
            src, dst = cks.at[CORNERS[d]], ck.at[CORNERS[(-dx, -dy)]]
        return remote(src, dst, c_send.at[here], c_recv.at[back], dx, dy)

    src1 = {-1: (3, 3), 0: (3, 8), 1: (8, 3)}
    dst1 = {-1: (0, 3), 0: (3, 8), 1: (11, 3)}
    qsrc1 = {-1: (1, 1), 0: (1, 2), 1: (2, 1)}
    qdst1 = {-1: (0, 1), 0: (1, 2), 1: (3, 1)}
    src2 = {-1: (3, 3), 0: (3, 4), 1: (4, 3)}
    dst2 = {-1: (0, 3), 0: (3, 4), 1: (7, 3)}

    def region1(rows, quads):
        return q1_v.at[pl.ds(*rows), pl.ds(*quads)]

    def region2(rows, quad):
        return q2_v.at[pl.ds(*rows), quad]

    def one_copy(d):
        dx, dy = d
        return remote(
            region1(src1[dx], qsrc1[dy]), region1(dst1[-dx], qdst1[-dy]),
            q1_send.at[DIRS.index(d)], q1_recv.at[DIRS.index((-dx, -dy))], dx, dy,
        )

    def two_copy(d):
        dx, dy = d
        return remote(
            region2(src2[dx], 1), region2(dst2[-dx], 1 - dy),
            q2_send.at[DIRS.index(d)], q2_recv.at[DIRS.index((-dx, -dy))], dx, dy,
        )

    def along_copy(b):
        k = REACH.index(b)
        return remote(
            q3_v.at[3, 3], q3_v.at[3, 3 - b], t_send.at[k], t_recv.at[REACH.index(-b)], 0, b
        )

    def across_copy(a):
        k = REACH.index(a)
        return remote(
            q3_v.at[3], q3_v.at[3 - a], t_send.at[6 + k], t_recv.at[6 + REACH.index(-a)], a, 0
        )

    def start(copy, d):
        @pl.when(exists(*d))
        def _():
            copy.start()

    def arrived(copy, d):
        @pl.when(exists(*d))
        def _():
            copy.wait_recv()

    def sent(copy, d):
        @pl.when(exists(*d))
        def _():
            copy.wait_send()

    def blank(ref, d):
        @pl.when(jnp.logical_not(exists(*d)))
        def _():
            ref[...] = jnp.zeros(ref.shape, ref.dtype)

    for d in DIRS:
        dx, dy = d
        if dy == 0:
            blank(nr.at[EDGES[d]], d)
            blank(cr.at[EDGES[d]], d)
        elif dx == 0:
            blank(nc.at[EDGES[d]], d)
            blank(cc.at[EDGES[d]], d)
        else:
            blank(nk.at[CORNERS[d]], d)
            blank(ck.at[CORNERS[d]], d)
        blank(region1(dst1[dx], qdst1[dy]), d)
        blank(region2(dst2[dx], 1 + dy), d)
    for b in REACH:
        blank(q3_v.at[3, 3 + b], (0, b))
    for a in REACH:
        blank(q3_v.at[3 + a], (a, 0))
    for level in range(5):
        for s in GAPS:
            coupling_v[level, pl.ds(s * 64, 64)] = jnp.zeros((64, 64), BF)

    for c in small_loads[:2]:
        c.wait()

    def scale_row(i, carry):
        for h in range(2):
            amp_low = amp_v[h, pl.ds(i * 16, 8), :]
            amp_high = amp_v[h, pl.ds(i * 16 + 8, 8), :]
            for r in range(NR_):
                low = rhs_v[h, pl.ds(i * 128 + r, 8, stride=8), :] * amp_low
                high = rhs_v[h, pl.ds(i * 128 + 64 + r, 8, stride=8), :] * amp_high
                value = jnp.concatenate([low, high], axis=0).astype(BF)
                s_v[r, i, :, pl.ds(h * 128, 128)] = value
                fw[h, pl.ds(pl.multiple_of((r * NI + i + 1) * WJ + 8, 8), 16), :] = value.astype(F32)
        return carry

    for c in range(4):
        loads[2 * c].wait()
        loads[2 * c + 1].wait()
        lax.fori_loop(4 * c, 4 * c + 4, scale_row, 0)
    for c in weight_loads:
        c.start()

    def near_pack(r, carry):
        for k, j in ((0, 0), (1, 15)):
            for h in range(2):
                base = (r * NI + 1) * WJ + 8 + j
                rows = [fw[h, pl.ds(base + 8 * WJ * t, 8, stride=WJ), :] for t in range(2)]
                ncs[k, r, :, pl.ds(h * 128, 128)] = jnp.concatenate(rows, axis=0).astype(BF)
        return carry

    lax.fori_loop(0, NR_, near_pack, 0)
    for (dx, dy), k in CORNERS.items():
        i, j = (0 if dx < 0 else 15), (0 if dy < 0 else 15)
        for h in range(2):
            nks[k, :, pl.ds(h * 128, 128)] = fw[
                h, pl.ds((i + 1) * WJ + 8 + j, 8, stride=NI * WJ), :
            ]
    pl.semaphore_wait(barrier, total)
    for d in DIRS:
        start(near_copy(d), d)

    for c in small_loads[2:]:
        c.wait()
    basis = basis_v[...]
    basis_twice = jnp.concatenate([basis, basis], axis=0)

    def leaf_level(r, carry):
        value = rounded(dot_t(s_v[r].reshape(256, 256), basis_twice))
        for i in range(16):
            cw[pl.ds(pl.multiple_of((r * WI + i + 3) * WJ + 8, 8), 16), :] = value[i * 16 : (i + 1) * 16]
        return carry

    lax.fori_loop(0, NR_, leaf_level, 0)

    def leaf_pack(r, carry):
        for k, first in ((0, 0), (1, 13)):
            for t in range(3):
                rows = [
                    cw[pl.ds(((r + u) * WI + 3 + first + t) * WJ + 8, 16), :] for u in (0, 4)
                ]
                crs[k, r, t] = sel(rows[0], rows[1]).astype(BF)
                cols = [
                    jnp.concatenate(
                        [
                            cw[
                                pl.ds(((r + u) * WI + 3 + 8 * v) * WJ + 8 + first + t, 8, stride=WJ),
                                :,
                            ]
                            for v in range(2)
                        ],
                        axis=0,
                    )
                    for u in (0, 4)
                ]
                ccs[k, r, t] = sel(cols[0], cols[1]).astype(BF)
        return carry

    lax.fori_loop(0, 4, leaf_pack, 0)

    def leaf_box(i, j):
        return cw[pl.ds(i * WJ + j, 8, stride=WI * WJ), :]

    for (dx, dy), k in CORNERS.items():
        first_i, first_j = (3 if dx < 0 else 16), (8 if dy < 0 else 21)
        for t in range(3):
            box = [leaf_box(first_i + t, first_j + u) for u in range(3)]
            cks[k, t] = jnp.concatenate([sel(box[0], box[2]), box[1]], axis=0).astype(BF)
    for d in DIRS:
        start(leaf_copy(d), d)

    def twice(level):
        t = transfer_v[level]
        return jnp.concatenate([t, t], axis=1)

    def gather_one(i, carry):
        for j in range(0, 8, 2):
            tiles = []
            for u in range(2):
                box = [
                    leaf_box(3 + 2 * i + a, 8 + 2 * (j + u) + b) for a in range(2) for b in range(2)
                ]
                tiles.append(
                    jnp.concatenate([sel(box[0], box[1]), sel(box[2], box[3])], axis=1)
                )
            u1_v[pl.ds(pl.multiple_of(i * 64 + j * 8, 16), 16), :] = jnp.concatenate(tiles, axis=0).astype(BF)
        return carry

    lax.fori_loop(0, 8, gather_one, 0)
    c1_v[...] = rounded(dot(u1_v[...], twice(0))).reshape(64, 8, 128)

    def quad_one(i, carry):
        for g in range(2):
            box = [c1_v[i * 8 + 4 * g + u] for u in range(4)]
            q1_v[3 + i, 1 + g] = jnp.concatenate(
                [sel(box[0], box[2]), sel(box[1], box[3])], axis=0
            ).astype(BF)
        return carry

    lax.fori_loop(0, 8, quad_one, 0)
    for d in DIRS:
        start(one_copy(d), d)

    def parents(children, n, i, j):
        box = [children[(2 * i + a) * 2 * n + 2 * j + b] for a in range(2) for b in range(2)]
        return jnp.concatenate([sel(box[0], box[1]), sel(box[2], box[3])], axis=1)

    def quad(box):
        return jnp.concatenate([sel(box[0], box[2]), sel(box[1], box[3])], axis=0).astype(BF)

    for i in range(4):
        for j in range(0, 4, 2):
            u2_v[pl.ds((i * 4 + j) * 8, 16), :] = jnp.concatenate(
                [parents(c1_v, 4, i, j + u) for u in range(2)], axis=0
            ).astype(BF)
    c2_v[...] = rounded(dot(u2_v[...], twice(1))).reshape(16, 8, 128)
    for i in range(4):
        q2_v[3 + i, 1] = quad([c2_v[i * 4 + u] for u in range(4)])
    for d in DIRS:
        start(two_copy(d), d)
    up = jnp.concatenate(
        [parents(c2_v, 2, i, j) for i in range(2) for j in range(2)], axis=0
    ).astype(BF)
    c3 = rounded(dot(up, twice(2)))
    q3_v[3, 3] = quad([c3[u * 8 : (u + 1) * 8] for u in range(4)])
    for b in REACH:
        start(along_copy(b), (0, b))

    for c in list_loads:
        c.wait()
    lists_v[...] = jnp.full(lists_v.shape, -1000000.0, F32)
    lists_v[pl.ds(0, 256), pl.ds(0, 27)] = f0_v[...].astype(F32)
    lists_v[pl.ds(256, 64), pl.ds(0, 27)] = f1_v[...].astype(F32)
    for i in range(4):
        lists_v[pl.ds(320 + 4 * i, 4), pl.ds(0, 27)] = f2_v[i].astype(F32)
    for i in range(2):
        lists_v[pl.ds(336 + 2 * i, 2), pl.ds(0, 27)] = f3_v[i].astype(F32)
    lists_v[pl.ds(340, 1), pl.ds(0, 27)] = f4_v[0].astype(F32)
    nlist_v[...] = jnp.full(nlist_v.shape, -1000000.0, F32)
    for s in range(9):
        nlist_v[pl.ds(16 * s, 16), pl.ds(0, 16)] = nl_v[s].astype(F32)

    far_t = jnp.concatenate(
        [jnp.transpose(lists_v[pl.ds(128 * t, 128), :])[0:32] for t in range(3)], axis=1
    )
    lane = lax.broadcasted_iota(jnp.int32, (1, 384), 1)
    level_of = [(0, 0, 16, 4), (256, 1, 8, 3), (320, 2, 4, 2), (336, 3, 2, 1), (340, 4, 1, 0)]
    base = jnp.zeros((1, 384), jnp.int32)
    pitch = jnp.zeros((1, 384), jnp.int32)
    for first, level, n, shift in level_of:
        local = lane - first
        cols = n * size_y
        mine = (x * n + lax.shift_right_arithmetic(local, shift)) * cols + y * n + (local & (n - 1))
        base = jnp.where(local >= 0, mine, base)
        pitch = jnp.where(local >= 0, cols, pitch)
    far_t = far_t - base.astype(F32)
    pitch = pitch.astype(F32)
    counts_v[...] = jnp.zeros(counts_v.shape, F32)

    def far_count(p, carry):
        row = (p - 3).astype(F32) * pitch
        for k, q in enumerate((-3, -2, -1, 0, 1, None, 2, 3)):
            if q is not None:
                hits = jnp.where(far_t == row + float(q), 1.0, 0.0)
                counts_v[pl.ds(p * 8 + k, 1), :] = jnp.sum(hits, axis=0, keepdims=True)
        return carry

    lax.fori_loop(0, 7, far_count, 0)
    near_t = []
    group = lax.broadcasted_iota(jnp.int32, (16, 128), 1) // 16
    for half in range(2):
        got = jnp.full((16, 128), -1000000.0, F32)
        for k in range(8):
            piece = nlist_v[pl.ds(half * 8 + k, 16, stride=16), :]
            if k:
                piece = pltpu.roll(piece, 16 * k, 1)
            got = jnp.where(group == k, piece, got)
        near_t.append(got)
    near_t = jnp.concatenate(near_t, axis=1) - base[:, 0:256].astype(F32)
    for o, (p, q) in enumerate(NEAR):
        hits = jnp.where(near_t == float(p) * float(16 * size_y) + float(q), 1.0, 0.0)
        counts_v[pl.ds(64 + o, 1), pl.ds(0, 256)] = jnp.sum(hits, axis=0, keepdims=True)
    counts = jnp.concatenate(
        [jnp.transpose(counts_v[:, pl.ds(128 * t, 128)]) for t in range(3)], axis=0
    ).astype(BF)
    source = lax.broadcasted_iota(jnp.int32, (128, 256), 0)
    column = lax.broadcasted_iota(jnp.int32, (128, 256), 1)
    half_of = (column // 64) % 2
    second = column >= 128
    for t in range(0, PAIR_COUNT, 2):
        k = [(p + 3) * 8 + 2 * m for p, m in PAIRS[t : t + 2]]
        spread = jnp.where(source == jnp.where(second, k[1], k[0]) + half_of, 1.0, 0.0).astype(BF)
        weights = dot(counts, spread)
        w0_v[:, pl.ds(128 * t, 256)] = weights[0:256].astype(BF)
        w14_v[t] = weights[256:384, 0:128]
        w14_v[t + 1] = weights[256:384, 128:256]
    for o in range(0, 10, 2):
        spread = jnp.where(source == jnp.where(second, 65 + o, 64 + o), 1.0, 0.0).astype(BF)
        wn_v[:, pl.ds(128 * o, 256)] = dot(counts[0:256], spread).astype(BF)

    for d in DIRS:
        arrived(near_copy((-d[0], -d[1])), d)

    def near_unpack(r, carry):
        for k, ii, jj in ((0, 0, 7), (1, 17, 24)):
            for h in range(2):
                fw[h, pl.ds(pl.multiple_of((r * NI + ii) * WJ + 8, 8), 16), :] = nr[
                    k, r, :, pl.ds(h * 128, 128)
                ].astype(F32)
                column = nc[k, r, :, pl.ds(h * 128, 128)].astype(F32)
                for t in range(2):
                    fw[h, pl.ds((r * NI + 1 + 8 * t) * WJ + jj, 8, stride=WJ), :] = column[
                        8 * t : 8 * t + 8
                    ]
        return carry

    lax.fori_loop(0, NR_, near_unpack, 0)
    for (dx, dy), k in CORNERS.items():
        ii, jj = (0 if dx < 0 else 17), (7 if dy < 0 else 24)
        for h in range(2):
            fw[h, pl.ds(ii * WJ + jj, 8, stride=NI * WJ), :] = nk[k, :, pl.ds(h * 128, 128)]
    for c in weight_loads:
        c.wait()

    def near_rows(i):
        columns = []
        for o, (p, q) in enumerate(NEAR):
            w = wn_v[pl.ds(pl.multiple_of(i * 16, 16), 16), pl.ds(128 * o, 128)]
            for h in range(2):
                tiles = []
                for r in range(NR_):
                    first = (r * NI + i + 1 + p) * WJ + 8 + q
                    if q == 0:
                        first = pl.multiple_of(first, 8)
                    tiles.append(fw[h, pl.ds(first, 16), :].astype(BF) * w)
                columns.append(jnp.concatenate(tiles, axis=0))
        return jnp.concatenate(columns, axis=1)

    def near_block(block, carry):
        left = jnp.concatenate([near_rows(block * NEAR_ROWS + u) for u in range(NEAR_ROWS)], axis=0)
        rows = pl.ds(pl.multiple_of(block * (128 * NEAR_ROWS), 128 * NEAR_ROWS), 128 * NEAR_ROWS)
        acc_v[rows, :] = dot(left, near_v[...]).astype(BF)
        pltpu.make_async_copy(acc_v.at[rows], near_out_h.at[rows], out_sem.at[0]).start()
        return carry

    lax.fori_loop(0, 16 // NEAR_ROWS, near_block, 0)

    for b in REACH:
        arrived(along_copy(-b), (0, b))
    for a in REACH:
        start(across_copy(a), (a, 0))

    for d in DIRS:
        arrived(leaf_copy((-d[0], -d[1])), d)

    def leaf_unpack(r, carry):
        for k in range(2):
            for t in range(3):
                row = cr[k, r, t].astype(F32)
                other = swap(row)
                column = cc[k, r, t].astype(F32)
                across = swap(column)
                ii = t + (0, 19)[k]
                jj = t + (5, 24)[k]
                for u, value, col in (
                    (0, sel(row, other), sel(column, across)),
                    (4, sel(other, row), sel(across, column)),
                ):
                    cw[pl.ds(pl.multiple_of(((r + u) * WI + ii) * WJ + 8, 8), 16), :] = value
                    for v in range(2):
                        cw[pl.ds(((r + u) * WI + 3 + 8 * v) * WJ + jj, 8, stride=WJ), :] = col[
                            8 * v : 8 * v + 8
                        ]
        return carry

    lax.fori_loop(0, 4, leaf_unpack, 0)
    for (dx, dy), k in CORNERS.items():
        for t in range(3):
            value = ck[k, t].astype(F32)
            other = swap(value)
            ii = t + (0 if dx < 0 else 19)
            for u in range(3):
                jj = u + (5 if dy < 0 else 24)
                rows = slice(8, 16) if u == 1 else slice(0, 8)
                box = sel(other, value) if u == 2 else sel(value, other)
                cw[pl.ds(ii * WJ + jj, 8, stride=WI * WJ), :] = box[rows]

    def pair_row(r, carry):
        for ii in range(WI):
            for m, q in enumerate(PAIR_Q):
                a = cw[pl.ds((r * WI + ii) * WJ + 8 + q, 16), :]
                b = cw[pl.ds((r * WI + ii) * WJ + 9 + q, 16), :]
                pairs_v[m, r * WI + ii] = sel(a, b).astype(BF)
        return carry

    lax.fori_loop(0, NR_, pair_row, 0)

    def leaf_rows(i):
        columns = []
        for t, (p, m) in enumerate(PAIRS):
            w = w0_v[pl.ds(pl.multiple_of(i * 16, 16), 16), pl.ds(128 * t, 128)]
            columns.append(
                jnp.concatenate(
                    [pairs_v[m, r * WI + i + 3 + p] * w for r in range(NR_)], axis=0
                )
            )
        return jnp.concatenate(columns, axis=1)

    def leaf_block(block, carry):
        left = jnp.concatenate([leaf_rows(block * LEAF_ROWS + u) for u in range(LEAF_ROWS)], axis=0)
        rows = pl.ds(pl.multiple_of(block * (128 * LEAF_ROWS), 128 * LEAF_ROWS), 128 * LEAF_ROWS)
        y0_v[rows, :] = dot(left, coupling_v[0])
        return carry

    lax.fori_loop(0, 16 // LEAF_ROWS, leaf_block, 0)

    for d in DIRS:
        arrived(one_copy((-d[0], -d[1])), d)
        arrived(two_copy((-d[0], -d[1])), d)
    for a in REACH:
        arrived(across_copy(-a), (a, 0))

    def quad_parts(value):
        value = value.astype(F32)
        low, high = value[0:8], value[8:16]
        return low, high, swap(low), swap(high)

    def quad_row(dst, row, quads, first, last):
        parts = [quad_parts(v) for v in quads]
        for g, (lo, hi, lo_s, hi_s) in enumerate(parts):
            values = [sel(lo, hi_s), sel(hi, lo), sel(lo_s, hi)]
            if g + 1 < len(parts):
                values.append(sel(hi_s, parts[g + 1][2]))
            for u, value in enumerate(values):
                col = 4 * g + u - 1
                if first <= col < last:
                    dst[row, col] = value

    def rows_one(i, carry):
        quad_row(d1_v, i, [q1_v[i, g] for g in range(4)], 0, 13)
        return carry

    for i in range(14):
        rows_one(i, 0)

    def rows_two(i, carry):
        quad_row(d2_v, i, [q2_v[i, g] for g in range(3)], 0, 9)
        return carry

    for i in range(10):
        rows_two(i, 0)

    for dev in range(7):
        parts = [quad_parts(q3_v[dev, g]) for g in range(7)]
        for a in range(2):
            if 3 <= 2 * dev + a <= 10:
                for col in range(7):
                    g, b = (col + 3) // 2, (col + 3) % 2
                    lo, hi, lo_s, hi_s = parts[g]
                    lo_n, _, lo_sn, _ = parts[g + 1]
                    if b == 0:
                        value = sel(lo, hi_s) if a == 0 else sel(lo_s, hi)
                    else:
                        value = sel(hi, lo_sn) if a == 0 else sel(hi_s, lo_n)
                    d3_v[2 * dev + a - 3, col] = value
        for g in range(7):
            lo, hi, lo_s, hi_s = parts[g]
            u4_v[dev, pl.ds(g * 8, 8), :] = jnp.concatenate([sel(lo, hi_s), sel(lo_s, hi)], axis=1)
    c4_v[...] = rounded(dot(u4_v[...].reshape(392, 256).astype(BF), twice(3))).reshape(7, 56, 128)
    for i in range(7):
        for j in range(6):
            d4_v[i, j] = sel(c4_v[i, pl.ds(8 * j, 8), :], c4_v[i, pl.ds(8 * j + 8, 8), :])

    def fill(dst, window, n, first):
        def two_boxes(h, carry):
            tiles = []
            places = []
            for u in range(2):
                b = h * 2 + u if n > 1 else 0
                places.append((b // n, b % n, first + b))
            for t, (p, m) in enumerate(PAIRS):
                tiles = []
                for i, j, b in places:
                    w = w14_v[t, pl.ds(b, 1), :]
                    tiles.append(window[i + 3 + p, j + 3 + PAIR_Q[m]] * jnp.broadcast_to(w, (8, 128)))
                dst[pl.ds(aligned(h * 16, 16), 16), pl.ds(128 * t, 128)] = jnp.concatenate(tiles, axis=0).astype(BF)
            return carry

        if n < 8:
            for h in range(max(1, n * n // 2)):
                two_boxes(h, 0)
        else:
            def four_boxes(h, carry):
                two_boxes(2 * h, carry)
                return two_boxes(2 * h + 1, carry)

            lax.fori_loop(0, n * n // 4, four_boxes, 0)

    fill(x4_v, d4_v, 1, 84)
    fill(x3_v, d3_v, 2, 80)
    fill(x2_v, d2_v, 4, 64)
    fill(x1_v, d1_v, 8, 0)
    down = dot(x4_v[...], coupling_v[4])[0:8].astype(BF)
    for level, n, xs, ys in ((3, 2, x3_v, y3_v), (2, 4, x2_v, y2_v), (1, 8, x1_v, y1_v)):
        ys[...] = dot(xs[...], coupling_v[level])
        for a in range(2):
            for b in range(2):
                spread = dot_t(down, transfer_v[level, pl.ds((2 * a + b) * 64, 64), :])
                for i in range(n // 2):
                    for j in range(n // 2):
                        at = ((2 * i + a) * n + 2 * j + b) * 8
                        part = (i * (n // 2) + j) * 8
                        ys[pl.ds(at, 8), :] += spread[part : part + 8]
        down = ys[...].astype(BF)
    for a in range(2):
        for b in range(2):
            t = transfer_v[0, pl.ds((2 * a + b) * 64, 64), :]
            spread = dot_t(down, jnp.concatenate([t, t], axis=0))
            for i in range(8):
                for j in range(8):
                    at = (2 * i + a) * 128 + 2 * j + b
                    part = (i * 8 + j) * 8
                    g_v[pl.ds(at, 8, stride=16), :] = spread[part : part + 8]

    d0_v[...] = (y0_v[...] + g_v[:, pl.ds(0, 64)]).astype(BF)
    leaf_out = pltpu.make_async_copy(d0_v, leaf_out_h, out_sem.at[1])
    leaf_out.start()
    for d in DIRS:
        for copy in (near_copy, leaf_copy, one_copy, two_copy):
            sent(copy(d), d)
    for b in REACH:
        sent(along_copy(b), (0, b))
    for a in REACH:
        sent(across_copy(a), (a, 0))
    pltpu.make_async_copy(acc_v, near_out_h, out_sem.at[0]).wait()
    leaf_out.wait()


def finish(near_ref, leaf_ref, basis_ref, amp_ref, out_ref):
    count = near_ref.shape[0] // 128
    far = jnp.dot(leaf_ref[...], basis_ref[...], preferred_element_type=F32)
    value = near_ref[...].astype(F32) + far
    for i in range(count):
        amp = amp_ref[pl.ds(i * 16, 16), :]
        rows = value[i * 128 : (i + 1) * 128].reshape(NR_, 16, 256) * amp[None]
        for v in range(2):
            part = jnp.swapaxes(rows[:, 8 * v : 8 * v + 8], 0, 1)
            out_ref[pl.ds(i * 128 + v * 64, 64), :] = part.reshape(64, 256)


def body(
    right_sides, amplitude, near_list, far_leaf, far_one, far_two, far_three, far_four,
    basis, transfer, coupling, near_tiles,
):
    size_x, size_y = lax.axis_size("bx"), lax.axis_size("by")
    dma = pltpu.SemaphoreType.DMA
    vmem = pltpu.VMEM
    i32 = jnp.int32
    operands = (
        right_sides.reshape(2048, 256), amplitude.reshape(256, 256),
        jnp.transpose(near_list, (2, 0, 1)), far_leaf.reshape(256, 27), far_one.reshape(64, 27),
        far_two, far_three, far_four, basis.T, transfer.reshape(4, 256, 64),
        coupling.reshape(5, 2560, 64), near_tiles.reshape(2304, 256),
    )
    scratch = [
        vmem((2, 2048, 128), F32), vmem((2, 256, 128), F32), vmem((9, 16, 16), i32),
        vmem((256, 27), i32), vmem((64, 27), i32), vmem((4, 4, 27), i32), vmem((2, 2, 27), i32),
        vmem((1, 1, 27), i32), vmem((64, 256), BF), vmem((4, 256, 64), BF),
        vmem((5, SLOTS * 64, 64), BF), vmem((2304, 256), BF),
        vmem((8, 16, 16, 256), BF), vmem((2, NR_ * NI * WJ, 128), F32),
        vmem((NR_ * WI * WJ, 128), F32), vmem((2048, 128), F32), vmem((4, NR_ * WI, 16, 128), BF),
        vmem((384, 128), F32), vmem((256, 128), F32), vmem((128, 384), F32),
        vmem((256, 10 * 128), BF), vmem((256, PAIR_COUNT * 128), BF), vmem((PAIR_COUNT, 128, 128), F32),
        vmem((2, 8, 16, 256), BF), vmem((4, 8, 256), F32),
        vmem((2, 8, 16, 256), BF), vmem((2, 8, 16, 256), BF), vmem((4, 8, 256), F32),
        vmem((2, 4, 3, 16, 128), BF), vmem((2, 4, 3, 16, 128), BF), vmem((4, 3, 16, 128), BF),
        vmem((2, 4, 3, 16, 128), BF), vmem((2, 4, 3, 16, 128), BF), vmem((4, 3, 16, 128), BF),
        vmem((512, 256), BF), vmem((64, 8, 128), F32), vmem((128, 256), BF), vmem((16, 8, 128), F32),
        vmem((14, 4, 16, 128), BF), vmem((10, 3, 16, 128), BF), vmem((7, 7, 16, 128), BF),
        vmem((7, 56, 256), F32), vmem((7, 56, 128), F32),
        vmem((14, 13, 8, 128), F32), vmem((10, 9, 8, 128), F32), vmem((8, 7, 8, 128), F32),
        vmem((7, 6, 8, 128), F32),
        vmem((512, SLOTS * 64), BF), vmem((128, SLOTS * 64), BF), vmem((32, SLOTS * 64), BF),
        vmem((16, SLOTS * 64), BF),
        vmem((512, 64), F32), vmem((128, 64), F32), vmem((32, 64), F32), vmem((16, 64), F32),
        vmem((2048, 256), BF), vmem((2048, 64), F32), vmem((2048, 64), BF),
        dma((12,)), dma((6,)), dma((6,)), dma((2,)),
        dma((8,)), dma((8,)), dma((8,)), dma((8,)), dma((8,)), dma((8,)), dma((8,)), dma((8,)),
        dma((12,)), dma((12,)),
    ]
    near, leaf = pl.pallas_call(
        functools.partial(kernel, size_x, size_y),
        out_shape=[jax.ShapeDtypeStruct((2048, 256), BF), jax.ShapeDtypeStruct((2048, 64), BF)],
        in_specs=[pl.BlockSpec(memory_space=pl.ANY)] * len(operands),
        out_specs=[pl.BlockSpec(memory_space=pl.ANY)] * 2,
        scratch_shapes=scratch,
        compiler_params=pltpu.CompilerParams(
            collective_id=0, has_side_effects=True, vmem_limit_bytes=56 * 1024 * 1024
        ),
        cost_estimate=pl.CostEstimate(
            flops=12_000_000_000, bytes_accessed=10_000_000, transcendentals=0
        ),
    )(*operands)
    steps = 4
    product = pl.pallas_call(
        finish,
        out_shape=jax.ShapeDtypeStruct((2048, 256), F32),
        grid=(steps,),
        in_specs=[
            pl.BlockSpec((2048 // steps, 256), lambda n: (n, 0)),
            pl.BlockSpec((2048 // steps, 64), lambda n: (n, 0)),
            pl.BlockSpec((64, 256), lambda n: (0, 0)),
            pl.BlockSpec((256 // steps, 256), lambda n: (n, 0)),
        ],
        out_specs=pl.BlockSpec((2048 // steps, 256), lambda n: (n, 0)),
        compiler_params=pltpu.CompilerParams(vmem_limit_bytes=16 * 1024 * 1024),
        cost_estimate=pl.CostEstimate(
            flops=100_000_000, bytes_accessed=4_000_000, transcendentals=0
        ),
    )(near, leaf, operands[8], operands[1])
    return product.reshape(right_sides.shape)


def solution(mesh):
    split3 = P("bx", "by", None)
    placed = (P("bx", "by", None, None),) + (split3,) * 7 + (P(),) * 4
    return jax.shard_map(
        body, mesh=mesh, in_specs=placed, out_specs=P("bx", "by", None, None), check_vma=False
    )
```

```python
import functools

import jax
import jax.numpy as jnp
from jax import lax
from jax.experimental import pallas as pl
from jax.experimental.pallas import tpu as pltpu
from jax.sharding import PartitionSpec as P

MESH = pl.DeviceIdType.MESH
F32 = jnp.float32
BF = jnp.bfloat16

DIRS = [(a, b) for a in (-1, 0, 1) for b in (-1, 0, 1) if (a, b) != (0, 0)]
EDGES = {(-1, 0): 0, (1, 0): 1, (0, -1): 0, (0, 1): 1}
CORNERS = {(-1, -1): 0, (-1, 1): 1, (1, -1): 2, (1, 1): 3}
REACH = (-3, -2, -1, 1, 2, 3)
NEAR = [(p, q) for p in (-1, 0, 1) for q in (-1, 0, 1)]
PAIR_Q = (-3, -1, 1, 2)
PAIRS = [
    (p, m) for p in range(-3, 4) for m in range(4) if abs(p) >= 2 or m in (0, 3)
]
PAIR_COUNT = len(PAIRS)
RUNS = ((0, 0, 5), (6, 5, 7), (14, 12, 19), (34, 31, 7), (42, 38, 2))
GAPS = (5, 13, 33, 41)
SLOTS = 44
NEAR_ROWS = 8
LEAF_ROWS = 8
PARTS = 4

NR_ = 8
WI = 22
WJ = 32
NI = 18


def low_half(shape):
    return lax.broadcasted_iota(jnp.int32, shape, len(shape) - 1) < 64


def sel(a, b):
    return jnp.where(low_half(a.shape), a, b)


def aligned(v, n):
    return v if isinstance(v, int) else pl.multiple_of(v, n)


def swap(v):
    return pltpu.roll(v, 64, 1)


def rounded(v):
    return v.astype(BF).astype(F32)


def dot(a, b):
    return jnp.dot(a, b, preferred_element_type=F32)


def dot_t(a, b):
    return lax.dot_general(a, b, (((1,), (1,)), ((), ())), preferred_element_type=F32)


def kernel(
    size_x, size_y,
    rhs_h, amp_h, nl_h, f0_h, f1_h, f2_h, f3_h, f4_h, basis_h, transfer_h, coupling_h, near_h,
    near_out_h, leaf_out_h,
    rhs_v, amp_v, nl_v, f0_v, f1_v, f2_v, f3_v, f4_v, basis_v, transfer_v, coupling_v, near_v,
    s_v, fw, cw, g_v, pairs_v,
    lists_v, nlist_v, counts_v, wn_v, w0_v, w14_v,
    ncs, nks, nr, nc, nk,
    crs, ccs, cks, cr, cc, ck,
    u1_v, c1_v, u2_v, c2_v, q1_v, q2_v, q3_v, u4_v, c4_v,
    d1_v, d2_v, d3_v, d4_v, x1_v, x2_v, x3_v, x4_v, y1_v, y2_v, y3_v, y4_v,
    acc_v, y0_v, d0_v,
    load_sem, list_sem, weight_sem, out_sem,
    n_send, n_recv, c_send, c_recv, q1_send, q1_recv, q2_send, q2_recv, t_send, t_recv,
):
    x = lax.axis_index("bx")
    y = lax.axis_index("by")

    def exists(dx, dy):
        ok = True
        tests = []
        if dx < 0:
            tests.append(x >= -dx)
        if dx > 0:
            tests.append(x < size_x - dx)
        if dy < 0:
            tests.append(y >= -dy)
        if dy > 0:
            tests.append(y < size_y - dy)
        ok = tests[0]
        for t in tests[1:]:
            ok = jnp.logical_and(ok, t)
        return ok

    loads = [
        pltpu.make_async_copy(
            rhs_h.at[pl.ds(c * 512, 512), pl.ds(h * 128, 128)],
            rhs_v.at[h, pl.ds(c * 512, 512)],
            load_sem.at[2 * c + h],
        )
        for c in range(4)
        for h in range(2)
    ]
    small_loads = [
        pltpu.make_async_copy(amp_h.at[:, pl.ds(h * 128, 128)], amp_v.at[h], load_sem.at[8 + h])
        for h in range(2)
    ] + [
        pltpu.make_async_copy(basis_h, basis_v, load_sem.at[10]),
        pltpu.make_async_copy(transfer_h, transfer_v, load_sem.at[11]),
    ]
    list_loads = [
        pltpu.make_async_copy(a, b, list_sem.at[n])
        for n, (a, b) in enumerate(
            ((nl_h, nl_v), (f0_h, f0_v), (f1_h, f1_v), (f2_h, f2_v), (f3_h, f3_v), (f4_h, f4_v))
        )
    ]
    weight_loads = [pltpu.make_async_copy(near_h, near_v, weight_sem.at[0])] + [
        pltpu.make_async_copy(
            coupling_h.at[:, pl.ds(o * 64, n * 64)],
            coupling_v.at[:, pl.ds(s * 64, n * 64)],
            weight_sem.at[1 + k],
        )
        for k, (s, o, n) in enumerate(RUNS)
    ]
    for c in small_loads[:2] + loads + small_loads[2:] + list_loads:
        c.start()

    barrier = pltpu.get_barrier_semaphore()
    partners = DIRS + [(0, b) for b in REACH if abs(b) > 1] + [(a, 0) for a in REACH if abs(a) > 1]
    total = jnp.int32(0)
    for dx, dy in partners:
        ok = exists(dx, dy)

        @pl.when(ok)
        def _():
            pl.semaphore_signal(
                barrier, inc=1, device_id=(x + dx, y + dy), device_id_type=MESH
            )

        total = total + jnp.where(ok, 1, 0).astype(jnp.int32)

    def remote(src, dst, ssem, rsem, dx, dy):
        return pltpu.make_async_remote_copy(
            src_ref=src, dst_ref=dst, send_sem=ssem, recv_sem=rsem,
            device_id=(x + dx, y + dy), device_id_type=MESH,
        )

    def near_copy(d):
        dx, dy = d
        back = DIRS.index((-dx, -dy))
        here = DIRS.index(d)
        if dy == 0:
            src, dst = s_v.at[:, 0 if dx < 0 else 15], nr.at[EDGES[(-dx, 0)]]
        elif dx == 0:
            src, dst = ncs.at[EDGES[d]], nc.at[EDGES[(0, -dy)]]
        else:
            src, dst = nks.at[CORNERS[d]], nk.at[CORNERS[(-dx, -dy)]]
        return remote(src, dst, n_send.at[here], n_recv.at[back], dx, dy)

    def leaf_copy(d):
        dx, dy = d
        back = DIRS.index((-dx, -dy))
        here = DIRS.index(d)
        if dy == 0:
            src, dst = crs.at[EDGES[d]], cr.at[EDGES[(-dx, 0)]]
        elif dx == 0:
            src, dst = ccs.at[EDGES[d]], cc.at[EDGES[(0, -dy)]]
        else:
            src, dst = cks.at[CORNERS[d]], ck.at[CORNERS[(-dx, -dy)]]
        return remote(src, dst, c_send.at[here], c_recv.at[back], dx, dy)

    src1 = {-1: (3, 3), 0: (3, 8), 1: (8, 3)}
    dst1 = {-1: (0, 3), 0: (3, 8), 1: (11, 3)}
    qsrc1 = {-1: (1, 1), 0: (1, 2), 1: (2, 1)}
    qdst1 = {-1: (0, 1), 0: (1, 2), 1: (3, 1)}
    src2 = {-1: (3, 3), 0: (3, 4), 1: (4, 3)}
    dst2 = {-1: (0, 3), 0: (3, 4), 1: (7, 3)}

    def region1(rows, quads):
        return q1_v.at[pl.ds(*rows), pl.ds(*quads)]

    def region2(rows, quad):
        return q2_v.at[pl.ds(*rows), quad]

    def one_copy(d):
        dx, dy = d
        return remote(
            region1(src1[dx], qsrc1[dy]), region1(dst1[-dx], qdst1[-dy]),
            q1_send.at[DIRS.index(d)], q1_recv.at[DIRS.index((-dx, -dy))], dx, dy,
        )

    def two_copy(d):
        dx, dy = d
        return remote(
            region2(src2[dx], 1), region2(dst2[-dx], 1 - dy),
            q2_send.at[DIRS.index(d)], q2_recv.at[DIRS.index((-dx, -dy))], dx, dy,
        )

    def along_copy(b):
        k = REACH.index(b)
        return remote(
            q3_v.at[3, 3], q3_v.at[3, 3 - b], t_send.at[k], t_recv.at[REACH.index(-b)], 0, b
        )

    def across_copy(a):
        k = REACH.index(a)
        return remote(
            q3_v.at[3], q3_v.at[3 - a], t_send.at[6 + k], t_recv.at[6 + REACH.index(-a)], a, 0
        )

    def start(copy, d):
        @pl.when(exists(*d))
        def _():
            copy.start()

    def arrived(copy, d):
        @pl.when(exists(*d))
        def _():
            copy.wait_recv()

    def sent(copy, d):
        @pl.when(exists(*d))
        def _():
            copy.wait_send()

    def blank(ref, d):
        @pl.when(jnp.logical_not(exists(*d)))
        def _():
            ref[...] = jnp.zeros(ref.shape, ref.dtype)

    for d in DIRS:
        dx, dy = d
        if dy == 0:
            blank(nr.at[EDGES[d]], d)
            blank(cr.at[EDGES[d]], d)
        elif dx == 0:
            blank(nc.at[EDGES[d]], d)
            blank(cc.at[EDGES[d]], d)
        else:
            blank(nk.at[CORNERS[d]], d)
            blank(ck.at[CORNERS[d]], d)
        blank(region1(dst1[dx], qdst1[dy]), d)
        blank(region2(dst2[dx], 1 + dy), d)
    for b in REACH:
        blank(q3_v.at[3, 3 + b], (0, b))
    for a in REACH:
        blank(q3_v.at[3 + a], (a, 0))
    for level in range(5):
        for s in GAPS:
            coupling_v[level, pl.ds(s * 64, 64)] = jnp.zeros((64, 64), BF)

    for c in small_loads[:2]:
        c.wait()

    def scale_row(i, carry):
        for h in range(2):
            amp_low = amp_v[h, pl.ds(i * 16, 8), :]
            amp_high = amp_v[h, pl.ds(i * 16 + 8, 8), :]
            for r in range(NR_):
                low = rhs_v[h, pl.ds(i * 128 + r, 8, stride=8), :] * amp_low
                high = rhs_v[h, pl.ds(i * 128 + 64 + r, 8, stride=8), :] * amp_high
                value = jnp.concatenate([low, high], axis=0).astype(BF)
                s_v[r, i, :, pl.ds(h * 128, 128)] = value
                fw[h, pl.ds(pl.multiple_of((r * NI + i + 1) * WJ + 8, 8), 16), :] = value.astype(F32)
        return carry

    for c in range(4):
        loads[2 * c].wait()
        loads[2 * c + 1].wait()
        lax.fori_loop(4 * c, 4 * c + 4, scale_row, 0)
    for c in weight_loads:
        c.start()

    def near_pack(r, carry):
        for k, j in ((0, 0), (1, 15)):
            for h in range(2):
                base = (r * NI + 1) * WJ + 8 + j
                rows = [fw[h, pl.ds(base + 8 * WJ * t, 8, stride=WJ), :] for t in range(2)]
                ncs[k, r, :, pl.ds(h * 128, 128)] = jnp.concatenate(rows, axis=0).astype(BF)
        return carry

    lax.fori_loop(0, NR_, near_pack, 0)
    for (dx, dy), k in CORNERS.items():
        i, j = (0 if dx < 0 else 15), (0 if dy < 0 else 15)
        for h in range(2):
            nks[k, :, pl.ds(h * 128, 128)] = fw[
                h, pl.ds((i + 1) * WJ + 8 + j, 8, stride=NI * WJ), :
            ]
    pl.semaphore_wait(barrier, total)
    for d in DIRS:
        start(near_copy(d), d)

    for c in small_loads[2:]:
        c.wait()
    basis = basis_v[...]
    basis_twice = jnp.concatenate([basis, basis], axis=0)

    def leaf_level(k, carry):
        value = rounded(dot_t(s_v[pl.ds(4 * k, 4)].reshape(1024, 256), basis_twice))
        for u in range(4):
            for i in range(16):
                row = ((4 * k + u) * WI + i + 3) * WJ + 8
                at = (u * 16 + i) * 16
                cw[pl.ds(pl.multiple_of(row, 8), 16), :] = value[at : at + 16]
        return carry

    lax.fori_loop(0, 2, leaf_level, 0)

    def leaf_pack(r, carry):
        for k, first in ((0, 0), (1, 13)):
            for t in range(3):
                rows = [
                    cw[pl.ds(((r + u) * WI + 3 + first + t) * WJ + 8, 16), :] for u in (0, 4)
                ]
                crs[k, r, t] = sel(rows[0], rows[1]).astype(BF)
                cols = [
                    jnp.concatenate(
                        [
                            cw[
                                pl.ds(((r + u) * WI + 3 + 8 * v) * WJ + 8 + first + t, 8, stride=WJ),
                                :,
                            ]
                            for v in range(2)
                        ],
                        axis=0,
                    )
                    for u in (0, 4)
                ]
                ccs[k, r, t] = sel(cols[0], cols[1]).astype(BF)
        return carry

    lax.fori_loop(0, 4, leaf_pack, 0)

    def leaf_box(i, j):
        return cw[pl.ds(i * WJ + j, 8, stride=WI * WJ), :]

    for (dx, dy), k in CORNERS.items():
        first_i, first_j = (3 if dx < 0 else 16), (8 if dy < 0 else 21)
        for t in range(3):
            box = [leaf_box(first_i + t, first_j + u) for u in range(3)]
            cks[k, t] = jnp.concatenate([sel(box[0], box[2]), box[1]], axis=0).astype(BF)
    for d in DIRS:
        start(leaf_copy(d), d)

    def twice(level):
        t = transfer_v[level]
        return jnp.concatenate([t, t], axis=1)

    def gather_one(i, carry):
        for j in range(0, 8, 2):
            tiles = []
            for u in range(2):
                box = [
                    leaf_box(3 + 2 * i + a, 8 + 2 * (j + u) + b) for a in range(2) for b in range(2)
                ]
                tiles.append(
                    jnp.concatenate([sel(box[0], box[1]), sel(box[2], box[3])], axis=1)
                )
            u1_v[pl.ds(pl.multiple_of(i * 64 + j * 8, 16), 16), :] = jnp.concatenate(tiles, axis=0).astype(BF)
        return carry

    lax.fori_loop(0, 8, gather_one, 0)
    c1_v[...] = rounded(dot(u1_v[...], twice(0))).reshape(64, 8, 128)

    def quad_one(i, carry):
        for g in range(2):
            box = [c1_v[i * 8 + 4 * g + u] for u in range(4)]
            q1_v[3 + i, 1 + g] = jnp.concatenate(
                [sel(box[0], box[2]), sel(box[1], box[3])], axis=0
            ).astype(BF)
        return carry

    lax.fori_loop(0, 8, quad_one, 0)
    for d in DIRS:
        start(one_copy(d), d)

    def parents(children, n, i, j):
        box = [children[(2 * i + a) * 2 * n + 2 * j + b] for a in range(2) for b in range(2)]
        return jnp.concatenate([sel(box[0], box[1]), sel(box[2], box[3])], axis=1)

    def quad(box):
        return jnp.concatenate([sel(box[0], box[2]), sel(box[1], box[3])], axis=0).astype(BF)

    for i in range(4):
        for j in range(0, 4, 2):
            u2_v[pl.ds((i * 4 + j) * 8, 16), :] = jnp.concatenate(
                [parents(c1_v, 4, i, j + u) for u in range(2)], axis=0
            ).astype(BF)
    c2_v[...] = rounded(dot(u2_v[...], twice(1))).reshape(16, 8, 128)
    for i in range(4):
        q2_v[3 + i, 1] = quad([c2_v[i * 4 + u] for u in range(4)])
    for d in DIRS:
        start(two_copy(d), d)
    up = jnp.concatenate(
        [parents(c2_v, 2, i, j) for i in range(2) for j in range(2)], axis=0
    ).astype(BF)
    c3 = rounded(dot(up, twice(2)))
    q3_v[3, 3] = quad([c3[u * 8 : (u + 1) * 8] for u in range(4)])
    for b in REACH:
        start(along_copy(b), (0, b))

    for c in list_loads:
        c.wait()
    lists_v[...] = jnp.full(lists_v.shape, -1000000.0, F32)
    lists_v[pl.ds(0, 256), pl.ds(0, 27)] = f0_v[...].astype(F32)
    lists_v[pl.ds(256, 64), pl.ds(0, 27)] = f1_v[...].astype(F32)
    for i in range(4):
        lists_v[pl.ds(320 + 4 * i, 4), pl.ds(0, 27)] = f2_v[i].astype(F32)
    for i in range(2):
        lists_v[pl.ds(336 + 2 * i, 2), pl.ds(0, 27)] = f3_v[i].astype(F32)
    lists_v[pl.ds(340, 1), pl.ds(0, 27)] = f4_v[0].astype(F32)
    nlist_v[...] = jnp.full(nlist_v.shape, -1000000.0, F32)
    for s in range(9):
        nlist_v[pl.ds(16 * s, 16), pl.ds(0, 16)] = nl_v[s].astype(F32)

    far_t = jnp.concatenate(
        [jnp.transpose(lists_v[pl.ds(128 * t, 128), :])[0:32] for t in range(3)], axis=1
    )
    lane = lax.broadcasted_iota(jnp.int32, (1, 384), 1)
    level_of = [(0, 0, 16, 4), (256, 1, 8, 3), (320, 2, 4, 2), (336, 3, 2, 1), (340, 4, 1, 0)]
    base = jnp.zeros((1, 384), jnp.int32)
    pitch = jnp.zeros((1, 384), jnp.int32)
    for first, level, n, shift in level_of:
        local = lane - first
        cols = n * size_y
        mine = (x * n + lax.shift_right_arithmetic(local, shift)) * cols + y * n + (local & (n - 1))
        base = jnp.where(local >= 0, mine, base)
        pitch = jnp.where(local >= 0, cols, pitch)
    far_t = far_t - base.astype(F32)
    pitch = pitch.astype(F32)
    counts_v[...] = jnp.zeros(counts_v.shape, F32)

    def far_count(p, carry):
        row = (p - 3).astype(F32) * pitch
        for k, q in enumerate((-3, -2, -1, 0, 1, None, 2, 3)):
            if q is not None:
                hits = jnp.where(far_t == row + float(q), 1.0, 0.0)
                counts_v[pl.ds(p * 8 + k, 1), :] = jnp.sum(hits, axis=0, keepdims=True)
        return carry

    lax.fori_loop(0, 7, far_count, 0)
    near_t = []
    group = lax.broadcasted_iota(jnp.int32, (16, 128), 1) // 16
    for half in range(2):
        got = jnp.full((16, 128), -1000000.0, F32)
        for k in range(8):
            piece = nlist_v[pl.ds(half * 8 + k, 16, stride=16), :]
            if k:
                piece = pltpu.roll(piece, 16 * k, 1)
            got = jnp.where(group == k, piece, got)
        near_t.append(got)
    near_t = jnp.concatenate(near_t, axis=1) - base[:, 0:256].astype(F32)
    for o, (p, q) in enumerate(NEAR):
        hits = jnp.where(near_t == float(p) * float(16 * size_y) + float(q), 1.0, 0.0)
        counts_v[pl.ds(64 + o, 1), pl.ds(0, 256)] = jnp.sum(hits, axis=0, keepdims=True)
    counts = jnp.concatenate(
        [jnp.transpose(counts_v[:, pl.ds(128 * t, 128)]) for t in range(3)], axis=0
    ).astype(BF)
    source = lax.broadcasted_iota(jnp.int32, (128, 256), 0)
    column = lax.broadcasted_iota(jnp.int32, (128, 256), 1)
    half_of = (column // 64) % 2
    second = column >= 128
    for t in range(0, PAIR_COUNT, 2):
        k = [(p + 3) * 8 + 2 * m for p, m in PAIRS[t : t + 2]]
        spread = jnp.where(source == jnp.where(second, k[1], k[0]) + half_of, 1.0, 0.0).astype(BF)
        weights = dot(counts, spread)
        w0_v[:, pl.ds(128 * t, 256)] = weights[0:256].astype(BF)
        w14_v[t] = weights[256:384, 0:128]
        w14_v[t + 1] = weights[256:384, 128:256]
    for o in range(0, 10, 2):
        spread = jnp.where(source == jnp.where(second, 65 + o, 64 + o), 1.0, 0.0).astype(BF)
        wn_v[:, pl.ds(128 * o, 256)] = dot(counts[0:256], spread).astype(BF)

    for d in DIRS:
        arrived(near_copy((-d[0], -d[1])), d)

    def near_unpack(r, carry):
        for k, ii, jj in ((0, 0, 7), (1, 17, 24)):
            for h in range(2):
                fw[h, pl.ds(pl.multiple_of((r * NI + ii) * WJ + 8, 8), 16), :] = nr[
                    k, r, :, pl.ds(h * 128, 128)
                ].astype(F32)
                column = nc[k, r, :, pl.ds(h * 128, 128)].astype(F32)
                for t in range(2):
                    fw[h, pl.ds((r * NI + 1 + 8 * t) * WJ + jj, 8, stride=WJ), :] = column[
                        8 * t : 8 * t + 8
                    ]
        return carry

    lax.fori_loop(0, NR_, near_unpack, 0)
    for (dx, dy), k in CORNERS.items():
        ii, jj = (0 if dx < 0 else 17), (7 if dy < 0 else 24)
        for h in range(2):
            fw[h, pl.ds(ii * WJ + jj, 8, stride=NI * WJ), :] = nk[k, :, pl.ds(h * 128, 128)]
    for c in weight_loads:
        c.wait()

    def near_rows(i):
        columns = []
        for o, (p, q) in enumerate(NEAR):
            w = wn_v[pl.ds(pl.multiple_of(i * 16, 16), 16), pl.ds(128 * o, 128)]
            for h in range(2):
                tiles = []
                for r in range(NR_):
                    first = (r * NI + i + 1 + p) * WJ + 8 + q
                    if q == 0:
                        first = pl.multiple_of(first, 8)
                    tiles.append(fw[h, pl.ds(first, 16), :].astype(BF) * w)
                columns.append(jnp.concatenate(tiles, axis=0))
        return jnp.concatenate(columns, axis=1)

    def near_block(block, carry):
        left = jnp.concatenate([near_rows(block * NEAR_ROWS + u) for u in range(NEAR_ROWS)], axis=0)
        rows = pl.ds(pl.multiple_of(block * (128 * NEAR_ROWS), 128 * NEAR_ROWS), 128 * NEAR_ROWS)
        acc_v[rows, :] = dot(left, near_v[...]).astype(BF)
        pltpu.make_async_copy(acc_v.at[rows], near_out_h.at[rows], out_sem.at[0]).start()
        return carry

    lax.fori_loop(0, 16 // NEAR_ROWS, near_block, 0)

    for b in REACH:
        arrived(along_copy(-b), (0, b))
    for a in REACH:
        start(across_copy(a), (a, 0))

    for d in DIRS:
        arrived(leaf_copy((-d[0], -d[1])), d)

    def leaf_unpack(r, carry):
        for k in range(2):
            for t in range(3):
                row = cr[k, r, t].astype(F32)
                other = swap(row)
                column = cc[k, r, t].astype(F32)
                across = swap(column)
                ii = t + (0, 19)[k]
                jj = t + (5, 24)[k]
                for u, value, col in (
                    (0, sel(row, other), sel(column, across)),
                    (4, sel(other, row), sel(across, column)),
                ):
                    cw[pl.ds(pl.multiple_of(((r + u) * WI + ii) * WJ + 8, 8), 16), :] = value
                    for v in range(2):
                        cw[pl.ds(((r + u) * WI + 3 + 8 * v) * WJ + jj, 8, stride=WJ), :] = col[
                            8 * v : 8 * v + 8
                        ]
        return carry

    lax.fori_loop(0, 4, leaf_unpack, 0)
    for (dx, dy), k in CORNERS.items():
        for t in range(3):
            value = ck[k, t].astype(F32)
            other = swap(value)
            ii = t + (0 if dx < 0 else 19)
            for u in range(3):
                jj = u + (5 if dy < 0 else 24)
                rows = slice(8, 16) if u == 1 else slice(0, 8)
                box = sel(other, value) if u == 2 else sel(value, other)
                cw[pl.ds(ii * WJ + jj, 8, stride=WI * WJ), :] = box[rows]

    def pair_row(r, carry):
        for ii in range(WI):
            for m, q in enumerate(PAIR_Q):
                a = cw[pl.ds((r * WI + ii) * WJ + 8 + q, 16), :]
                b = cw[pl.ds((r * WI + ii) * WJ + 9 + q, 16), :]
                pairs_v[m, r * WI + ii] = sel(a, b).astype(BF)
        return carry

    lax.fori_loop(0, NR_, pair_row, 0)

    def leaf_rows(i):
        columns = []
        for t, (p, m) in enumerate(PAIRS):
            w = w0_v[pl.ds(pl.multiple_of(i * 16, 16), 16), pl.ds(128 * t, 128)]
            columns.append(
                jnp.concatenate(
                    [pairs_v[m, r * WI + i + 3 + p] * w for r in range(NR_)], axis=0
                )
            )
        return jnp.concatenate(columns, axis=1)

    def leaf_block(block, carry):
        left = jnp.concatenate([leaf_rows(block * LEAF_ROWS + u) for u in range(LEAF_ROWS)], axis=0)
        rows = pl.ds(pl.multiple_of(block * (128 * LEAF_ROWS), 128 * LEAF_ROWS), 128 * LEAF_ROWS)
        y0_v[rows, :] = dot(left, coupling_v[0])
        return carry

    lax.fori_loop(0, 16 // LEAF_ROWS, leaf_block, 0)

    for d in DIRS:
        arrived(one_copy((-d[0], -d[1])), d)
        arrived(two_copy((-d[0], -d[1])), d)
    for a in REACH:
        arrived(across_copy(-a), (a, 0))

    def quad_parts(value):
        value = value.astype(F32)
        low, high = value[0:8], value[8:16]
        return low, high, swap(low), swap(high)

    def quad_row(dst, row, quads, first, last):
        parts = [quad_parts(v) for v in quads]
        for g, (lo, hi, lo_s, hi_s) in enumerate(parts):
            values = [sel(lo, hi_s), sel(hi, lo), sel(lo_s, hi)]
            if g + 1 < len(parts):
                values.append(sel(hi_s, parts[g + 1][2]))
            for u, value in enumerate(values):
                col = 4 * g + u - 1
                if first <= col < last:
                    dst[row, col] = value

    def rows_one(i, carry):
        quad_row(d1_v, i, [q1_v[i, g] for g in range(4)], 0, 13)
        return carry

    for i in range(14):
        rows_one(i, 0)

    def rows_two(i, carry):
        quad_row(d2_v, i, [q2_v[i, g] for g in range(3)], 0, 9)
        return carry

    for i in range(10):
        rows_two(i, 0)

    for dev in range(7):
        parts = [quad_parts(q3_v[dev, g]) for g in range(7)]
        for a in range(2):
            if 3 <= 2 * dev + a <= 10:
                for col in range(7):
                    g, b = (col + 3) // 2, (col + 3) % 2
                    lo, hi, lo_s, hi_s = parts[g]
                    lo_n, _, lo_sn, _ = parts[g + 1]
                    if b == 0:
                        value = sel(lo, hi_s) if a == 0 else sel(lo_s, hi)
                    else:
                        value = sel(hi, lo_sn) if a == 0 else sel(hi_s, lo_n)
                    d3_v[2 * dev + a - 3, col] = value
        for g in range(7):
            lo, hi, lo_s, hi_s = parts[g]
            u4_v[dev, pl.ds(g * 8, 8), :] = jnp.concatenate([sel(lo, hi_s), sel(lo_s, hi)], axis=1)
    c4_v[...] = rounded(dot(u4_v[...].reshape(392, 256).astype(BF), twice(3))).reshape(7, 56, 128)
    for i in range(7):
        for j in range(6):
            d4_v[i, j] = sel(c4_v[i, pl.ds(8 * j, 8), :], c4_v[i, pl.ds(8 * j + 8, 8), :])

    def fill(dst, window, n, first):
        def two_boxes(h, carry):
            tiles = []
            places = []
            for u in range(2):
                b = h * 2 + u if n > 1 else 0
                places.append((b // n, b % n, first + b))
            for t, (p, m) in enumerate(PAIRS):
                tiles = []
                for i, j, b in places:
                    w = w14_v[t, pl.ds(b, 1), :]
                    tiles.append(window[i + 3 + p, j + 3 + PAIR_Q[m]] * jnp.broadcast_to(w, (8, 128)))
                dst[pl.ds(aligned(h * 16, 16), 16), pl.ds(128 * t, 128)] = jnp.concatenate(tiles, axis=0).astype(BF)
            return carry

        if n < 8:
            for h in range(max(1, n * n // 2)):
                two_boxes(h, 0)
        else:
            def four_boxes(h, carry):
                two_boxes(2 * h, carry)
                return two_boxes(2 * h + 1, carry)

            lax.fori_loop(0, n * n // 4, four_boxes, 0)

    fill(x4_v, d4_v, 1, 84)
    fill(x3_v, d3_v, 2, 80)
    fill(x2_v, d2_v, 4, 64)
    fill(x1_v, d1_v, 8, 0)
    down = dot(x4_v[...], coupling_v[4])[0:8].astype(BF)
    for level, n, xs, ys in ((3, 2, x3_v, y3_v), (2, 4, x2_v, y2_v), (1, 8, x1_v, y1_v)):
        ys[...] = dot(xs[...], coupling_v[level])
        for a in range(2):
            for b in range(2):
                spread = dot_t(down, transfer_v[level, pl.ds((2 * a + b) * 64, 64), :])
                for i in range(n // 2):
                    for j in range(n // 2):
                        at = ((2 * i + a) * n + 2 * j + b) * 8
                        part = (i * (n // 2) + j) * 8
                        ys[pl.ds(at, 8), :] += spread[part : part + 8]
        down = ys[...].astype(BF)
    for a in range(2):
        for b in range(2):
            t = transfer_v[0, pl.ds((2 * a + b) * 64, 64), :]
            spread = dot_t(down, jnp.concatenate([t, t], axis=0))
            for i in range(8):
                for j in range(8):
                    at = (2 * i + a) * 128 + 2 * j + b
                    part = (i * 8 + j) * 8
                    g_v[pl.ds(at, 8, stride=16), :] = spread[part : part + 8]

    d0_v[...] = (y0_v[...] + g_v[:, pl.ds(0, 64)]).astype(BF)
    leaf_out = pltpu.make_async_copy(d0_v, leaf_out_h, out_sem.at[1])
    leaf_out.start()
    for d in DIRS:
        for copy in (near_copy, leaf_copy, one_copy, two_copy):
            sent(copy(d), d)
    for b in REACH:
        sent(along_copy(b), (0, b))
    for a in REACH:
        sent(across_copy(a), (a, 0))
    pltpu.make_async_copy(acc_v, near_out_h, out_sem.at[0]).wait()
    leaf_out.wait()


def finish(
    near_h, leaf_h, basis_h, amp_h, out_h, near_v, leaf_v, basis_v, amp_v, out_v, load_sem, out_sem
):
    small = [
        pltpu.make_async_copy(amp_h, amp_v, load_sem.at[0]),
        pltpu.make_async_copy(basis_h, basis_v, load_sem.at[1]),
    ]
    size = 2048 // PARTS
    parts = [pl.ds(n * size, size) for n in range(PARTS)]
    leaf = [
        pltpu.make_async_copy(leaf_h.at[p], leaf_v.at[p], load_sem.at[2 + n])
        for n, p in enumerate(parts)
    ]
    near = [
        pltpu.make_async_copy(near_h.at[p], near_v.at[p], load_sem.at[2 + PARTS + n])
        for n, p in enumerate(parts)
    ]
    outs = [
        pltpu.make_async_copy(out_v.at[p], out_h.at[p], out_sem.at[n]) for n, p in enumerate(parts)
    ]
    for n in range(PARTS):
        leaf[n].start()
        near[n].start()
        if n == 0:
            for c in small:
                c.start()
    for c in small:
        c.wait()
    for n, p in enumerate(parts):
        leaf[n].wait()
        far = dot(leaf_v[p, :], basis_v[...])
        near[n].wait()
        value = near_v[p, :].astype(F32) + far
        for i in range(size // 128):
            first = n * size + i * 128
            amp = amp_v[pl.ds(first // 8, 16), :]
            rows = value[i * 128 : (i + 1) * 128].reshape(NR_, 16, 256) * amp[None]
            for v in range(2):
                part = jnp.swapaxes(rows[:, 8 * v : 8 * v + 8], 0, 1)
                out_v[pl.ds(first + v * 64, 64), :] = part.reshape(64, 256)
        outs[n].start()
    for c in outs:
        c.wait()


def body(
    right_sides, amplitude, near_list, far_leaf, far_one, far_two, far_three, far_four,
    basis, transfer, coupling, near_tiles,
):
    size_x, size_y = lax.axis_size("bx"), lax.axis_size("by")
    dma = pltpu.SemaphoreType.DMA
    vmem = pltpu.VMEM
    i32 = jnp.int32
    operands = (
        right_sides.reshape(2048, 256), amplitude.reshape(256, 256),
        jnp.transpose(near_list, (2, 0, 1)), far_leaf.reshape(256, 27), far_one.reshape(64, 27),
        far_two, far_three, far_four, basis.T, transfer.reshape(4, 256, 64),
        coupling.reshape(5, 2560, 64), near_tiles.reshape(2304, 256),
    )
    scratch = [
        vmem((2, 2048, 128), F32), vmem((2, 256, 128), F32), vmem((9, 16, 16), i32),
        vmem((256, 27), i32), vmem((64, 27), i32), vmem((4, 4, 27), i32), vmem((2, 2, 27), i32),
        vmem((1, 1, 27), i32), vmem((64, 256), BF), vmem((4, 256, 64), BF),
        vmem((5, SLOTS * 64, 64), BF), vmem((2304, 256), BF),
        vmem((8, 16, 16, 256), BF), vmem((2, NR_ * NI * WJ, 128), F32),
        vmem((NR_ * WI * WJ, 128), F32), vmem((2048, 128), F32), vmem((4, NR_ * WI, 16, 128), BF),
        vmem((384, 128), F32), vmem((256, 128), F32), vmem((128, 384), F32),
        vmem((256, 10 * 128), BF), vmem((256, PAIR_COUNT * 128), BF), vmem((PAIR_COUNT, 128, 128), F32),
        vmem((2, 8, 16, 256), BF), vmem((4, 8, 256), F32),
        vmem((2, 8, 16, 256), BF), vmem((2, 8, 16, 256), BF), vmem((4, 8, 256), F32),
        vmem((2, 4, 3, 16, 128), BF), vmem((2, 4, 3, 16, 128), BF), vmem((4, 3, 16, 128), BF),
        vmem((2, 4, 3, 16, 128), BF), vmem((2, 4, 3, 16, 128), BF), vmem((4, 3, 16, 128), BF),
        vmem((512, 256), BF), vmem((64, 8, 128), F32), vmem((128, 256), BF), vmem((16, 8, 128), F32),
        vmem((14, 4, 16, 128), BF), vmem((10, 3, 16, 128), BF), vmem((7, 7, 16, 128), BF),
        vmem((7, 56, 256), F32), vmem((7, 56, 128), F32),
        vmem((14, 13, 8, 128), F32), vmem((10, 9, 8, 128), F32), vmem((8, 7, 8, 128), F32),
        vmem((7, 6, 8, 128), F32),
        vmem((512, SLOTS * 64), BF), vmem((128, SLOTS * 64), BF), vmem((32, SLOTS * 64), BF),
        vmem((16, SLOTS * 64), BF),
        vmem((512, 64), F32), vmem((128, 64), F32), vmem((32, 64), F32), vmem((16, 64), F32),
        vmem((2048, 256), BF), vmem((2048, 64), F32), vmem((2048, 64), BF),
        dma((12,)), dma((6,)), dma((6,)), dma((2,)),
        dma((8,)), dma((8,)), dma((8,)), dma((8,)), dma((8,)), dma((8,)), dma((8,)), dma((8,)),
        dma((12,)), dma((12,)),
    ]
    near, leaf = pl.pallas_call(
        functools.partial(kernel, size_x, size_y),
        out_shape=[jax.ShapeDtypeStruct((2048, 256), BF), jax.ShapeDtypeStruct((2048, 64), BF)],
        in_specs=[pl.BlockSpec(memory_space=pl.ANY)] * len(operands),
        out_specs=[pl.BlockSpec(memory_space=pl.ANY)] * 2,
        scratch_shapes=scratch,
        compiler_params=pltpu.CompilerParams(
            collective_id=0, has_side_effects=True, vmem_limit_bytes=56 * 1024 * 1024
        ),
        cost_estimate=pl.CostEstimate(
            flops=12_000_000_000, bytes_accessed=10_000_000, transcendentals=0
        ),
    )(*operands)
    product = pl.pallas_call(
        finish,
        out_shape=jax.ShapeDtypeStruct((2048, 256), F32),
        in_specs=[pl.BlockSpec(memory_space=pl.ANY)] * 4,
        out_specs=pl.BlockSpec(memory_space=pl.ANY),
        scratch_shapes=[
            vmem((2048, 256), BF), vmem((2048, 64), BF), vmem((64, 256), BF), vmem((256, 256), F32),
            vmem((2048, 256), F32), dma((2 + 2 * PARTS,)), dma((PARTS,)),
        ],
        compiler_params=pltpu.CompilerParams(vmem_limit_bytes=60 * 1024 * 1024),
        cost_estimate=pl.CostEstimate(
            flops=100_000_000, bytes_accessed=4_000_000, transcendentals=0
        ),
    )(near, leaf, operands[8], operands[1])
    return product.reshape(right_sides.shape)


def solution(mesh):
    split3 = P("bx", "by", None)
    placed = (P("bx", "by", None, None),) + (split3,) * 7 + (P(),) * 4
    return jax.shard_map(
        body, mesh=mesh, in_specs=placed, out_specs=P("bx", "by", None, None), check_vma=False
    )
```

```python
import functools

import jax
import jax.numpy as jnp
from jax import lax
from jax.experimental import pallas as pl
from jax.experimental.pallas import tpu as pltpu
from jax.sharding import PartitionSpec as P

MESH = pl.DeviceIdType.MESH
F32 = jnp.float32
BF = jnp.bfloat16

DIRS = [(a, b) for a in (-1, 0, 1) for b in (-1, 0, 1) if (a, b) != (0, 0)]
EDGES = {(-1, 0): 0, (1, 0): 1, (0, -1): 0, (0, 1): 1}
CORNERS = {(-1, -1): 0, (-1, 1): 1, (1, -1): 2, (1, 1): 3}
REACH = (-3, -2, -1, 1, 2, 3)
NEAR = [(p, q) for p in (-1, 0, 1) for q in (-1, 0, 1)]
PAIR_Q = (-3, -1, 1, 2)
PAIRS = [
    (p, m) for p in range(-3, 4) for m in range(4) if abs(p) >= 2 or m in (0, 3)
]
PAIR_COUNT = len(PAIRS)
RUNS = ((0, 0, 5), (6, 5, 7), (14, 12, 19), (34, 31, 7), (42, 38, 2))
GAPS = (5, 13, 33, 41)
SLOTS = 44
NEAR_ROWS = 8
LEAF_ROWS = 8
PARTS = 4

NR_ = 8
WI = 22
WJ = 32
NI = 18


def low_half(shape):
    return lax.broadcasted_iota(jnp.int32, shape, len(shape) - 1) < 64


def sel(a, b):
    return jnp.where(low_half(a.shape), a, b)


def aligned(v, n):
    return v if isinstance(v, int) else pl.multiple_of(v, n)


def swap(v):
    return pltpu.roll(v, 64, 1)


def rounded(v):
    return v.astype(BF).astype(F32)


def dot(a, b):
    return jnp.dot(a, b, preferred_element_type=F32)


def dot_t(a, b):
    return lax.dot_general(a, b, (((1,), (1,)), ((), ())), preferred_element_type=F32)


def kernel(
    size_x, size_y,
    rhs_h, amp_h, nl_h, f0_h, f1_h, f2_h, f3_h, f4_h, basis_h, transfer_h, coupling_h, near_h,
    near_out_h, leaf_out_h,
    rhs_v, amp_v, nl_v, f0_v, f1_v, f2_v, f3_v, f4_v, basis_v, transfer_v, coupling_v, near_v,
    s_v, fw, cw, g_v, pairs_v,
    lists_v, nlist_v, counts_v, wn_v, w0_v, w14_v,
    ncs, nks, nr, nc, nk,
    crs, ccs, cks, cr, cc, ck,
    u1_v, c1_v, u2_v, c2_v, q1_v, q2_v, q3_v, u4_v, c4_v,
    d1_v, d2_v, d3_v, d4_v, x1_v, x2_v, x3_v, x4_v, y1_v, y2_v, y3_v, y4_v,
    acc_v, y0_v, d0_v,
    load_sem, list_sem, weight_sem, out_sem,
    n_send, n_recv, c_send, c_recv, q1_send, q1_recv, q2_send, q2_recv, t_send, t_recv,
):
    x = lax.axis_index("bx")
    y = lax.axis_index("by")

    def exists(dx, dy):
        ok = True
        tests = []
        if dx < 0:
            tests.append(x >= -dx)
        if dx > 0:
            tests.append(x < size_x - dx)
        if dy < 0:
            tests.append(y >= -dy)
        if dy > 0:
            tests.append(y < size_y - dy)
        ok = tests[0]
        for t in tests[1:]:
            ok = jnp.logical_and(ok, t)
        return ok

    loads = [
        pltpu.make_async_copy(
            rhs_h.at[pl.ds(c * 512, 512), pl.ds(h * 128, 128)],
            rhs_v.at[h, pl.ds(c * 512, 512)],
            load_sem.at[2 * c + h],
        )
        for c in range(4)
        for h in range(2)
    ]
    small_loads = [
        pltpu.make_async_copy(amp_h.at[:, pl.ds(h * 128, 128)], amp_v.at[h], load_sem.at[8 + h])
        for h in range(2)
    ] + [
        pltpu.make_async_copy(basis_h, basis_v, load_sem.at[10]),
        pltpu.make_async_copy(transfer_h, transfer_v, load_sem.at[11]),
    ]
    list_loads = [
        pltpu.make_async_copy(a, b, list_sem.at[n])
        for n, (a, b) in enumerate(
            ((nl_h, nl_v), (f0_h, f0_v), (f1_h, f1_v), (f2_h, f2_v), (f3_h, f3_v), (f4_h, f4_v))
        )
    ]
    weight_loads = [pltpu.make_async_copy(near_h, near_v, weight_sem.at[0])] + [
        pltpu.make_async_copy(
            coupling_h.at[:, pl.ds(o * 64, n * 64)],
            coupling_v.at[:, pl.ds(s * 64, n * 64)],
            weight_sem.at[1 + k],
        )
        for k, (s, o, n) in enumerate(RUNS)
    ]
    for c in small_loads[:2] + loads + small_loads[2:] + list_loads:
        c.start()

    barrier = pltpu.get_barrier_semaphore()
    partners = DIRS + [(0, b) for b in REACH if abs(b) > 1] + [(a, 0) for a in REACH if abs(a) > 1]
    total = jnp.int32(0)
    for dx, dy in partners:
        ok = exists(dx, dy)

        @pl.when(ok)
        def _():
            pl.semaphore_signal(
                barrier, inc=1, device_id=(x + dx, y + dy), device_id_type=MESH
            )

        total = total + jnp.where(ok, 1, 0).astype(jnp.int32)

    def remote(src, dst, ssem, rsem, dx, dy):
        return pltpu.make_async_remote_copy(
            src_ref=src, dst_ref=dst, send_sem=ssem, recv_sem=rsem,
            device_id=(x + dx, y + dy), device_id_type=MESH,
        )

    def near_copy(d):
        dx, dy = d
        back = DIRS.index((-dx, -dy))
        here = DIRS.index(d)
        if dy == 0:
            src, dst = s_v.at[:, 0 if dx < 0 else 15], nr.at[EDGES[(-dx, 0)]]
        elif dx == 0:
            src, dst = ncs.at[EDGES[d]], nc.at[EDGES[(0, -dy)]]
        else:
            src, dst = nks.at[CORNERS[d]], nk.at[CORNERS[(-dx, -dy)]]
        return remote(src, dst, n_send.at[here], n_recv.at[back], dx, dy)

    def leaf_copy(d):
        dx, dy = d
        back = DIRS.index((-dx, -dy))
        here = DIRS.index(d)
        if dy == 0:
            src, dst = crs.at[EDGES[d]], cr.at[EDGES[(-dx, 0)]]
        elif dx == 0:
            src, dst = ccs.at[EDGES[d]], cc.at[EDGES[(0, -dy)]]
        else:
            src, dst = cks.at[CORNERS[d]], ck.at[CORNERS[(-dx, -dy)]]
        return remote(src, dst, c_send.at[here], c_recv.at[back], dx, dy)

    src1 = {-1: (3, 3), 0: (3, 8), 1: (8, 3)}
    dst1 = {-1: (0, 3), 0: (3, 8), 1: (11, 3)}
    qsrc1 = {-1: (1, 1), 0: (1, 2), 1: (2, 1)}
    qdst1 = {-1: (0, 1), 0: (1, 2), 1: (3, 1)}
    src2 = {-1: (3, 3), 0: (3, 4), 1: (4, 3)}
    dst2 = {-1: (0, 3), 0: (3, 4), 1: (7, 3)}

    def region1(rows, quads):
        return q1_v.at[pl.ds(*rows), pl.ds(*quads)]

    def region2(rows, quad):
        return q2_v.at[pl.ds(*rows), quad]

    def one_copy(d):
        dx, dy = d
        return remote(
            region1(src1[dx], qsrc1[dy]), region1(dst1[-dx], qdst1[-dy]),
            q1_send.at[DIRS.index(d)], q1_recv.at[DIRS.index((-dx, -dy))], dx, dy,
        )

    def two_copy(d):
        dx, dy = d
        return remote(
            region2(src2[dx], 1), region2(dst2[-dx], 1 - dy),
            q2_send.at[DIRS.index(d)], q2_recv.at[DIRS.index((-dx, -dy))], dx, dy,
        )

    def along_copy(b):
        k = REACH.index(b)
        return remote(
            q3_v.at[3, 3], q3_v.at[3, 3 - b], t_send.at[k], t_recv.at[REACH.index(-b)], 0, b
        )

    def across_copy(a):
        k = REACH.index(a)
        return remote(
            q3_v.at[3], q3_v.at[3 - a], t_send.at[6 + k], t_recv.at[6 + REACH.index(-a)], a, 0
        )

    def start(copy, d):
        @pl.when(exists(*d))
        def _():
            copy.start()

    def arrived(copy, d):
        @pl.when(exists(*d))
        def _():
            copy.wait_recv()

    def sent(copy, d):
        @pl.when(exists(*d))
        def _():
            copy.wait_send()

    def blank(ref, d):
        @pl.when(jnp.logical_not(exists(*d)))
        def _():
            ref[...] = jnp.zeros(ref.shape, ref.dtype)

    for d in DIRS:
        dx, dy = d
        if dy == 0:
            blank(nr.at[EDGES[d]], d)
            blank(cr.at[EDGES[d]], d)
        elif dx == 0:
            blank(nc.at[EDGES[d]], d)
            blank(cc.at[EDGES[d]], d)
        else:
            blank(nk.at[CORNERS[d]], d)
            blank(ck.at[CORNERS[d]], d)
        blank(region1(dst1[dx], qdst1[dy]), d)
        blank(region2(dst2[dx], 1 + dy), d)
    for b in REACH:
        blank(q3_v.at[3, 3 + b], (0, b))
    for a in REACH:
        blank(q3_v.at[3 + a], (a, 0))
    for level in range(5):
        for s in GAPS:
            coupling_v[level, pl.ds(s * 64, 64)] = jnp.zeros((64, 64), BF)

    for c in small_loads[:2]:
        c.wait()

    def scale_row(i, carry):
        for h in range(2):
            amp_low = amp_v[h, pl.ds(i * 16, 8), :]
            amp_high = amp_v[h, pl.ds(i * 16 + 8, 8), :]
            for r in range(NR_):
                low = rhs_v[h, pl.ds(i * 128 + r, 8, stride=8), :] * amp_low
                high = rhs_v[h, pl.ds(i * 128 + 64 + r, 8, stride=8), :] * amp_high
                value = jnp.concatenate([low, high], axis=0).astype(BF)
                s_v[r, i, :, pl.ds(h * 128, 128)] = value
                fw[h, pl.ds(pl.multiple_of((r * NI + i + 1) * WJ + 8, 8), 16), :] = value.astype(F32)
        return carry

    for c in range(4):
        loads[2 * c].wait()
        loads[2 * c + 1].wait()
        lax.fori_loop(4 * c, 4 * c + 4, scale_row, 0)
    for c in weight_loads:
        c.start()

    def near_pack(r, carry):
        for k, j in ((0, 0), (1, 15)):
            for h in range(2):
                base = (r * NI + 1) * WJ + 8 + j
                rows = [fw[h, pl.ds(base + 8 * WJ * t, 8, stride=WJ), :] for t in range(2)]
                ncs[k, r, :, pl.ds(h * 128, 128)] = jnp.concatenate(rows, axis=0).astype(BF)
        return carry

    lax.fori_loop(0, NR_, near_pack, 0)
    for (dx, dy), k in CORNERS.items():
        i, j = (0 if dx < 0 else 15), (0 if dy < 0 else 15)
        for h in range(2):
            nks[k, :, pl.ds(h * 128, 128)] = fw[
                h, pl.ds((i + 1) * WJ + 8 + j, 8, stride=NI * WJ), :
            ]
    pl.semaphore_wait(barrier, total)
    for d in DIRS:
        start(near_copy(d), d)

    for c in small_loads[2:]:
        c.wait()
    basis = basis_v[...]
    basis_twice = jnp.concatenate([basis, basis], axis=0)

    def leaf_level(k, carry):
        value = rounded(dot_t(s_v[pl.ds(4 * k, 4)].reshape(1024, 256), basis_twice))
        for u in range(4):
            for i in range(16):
                row = ((4 * k + u) * WI + i + 3) * WJ + 8
                at = (u * 16 + i) * 16
                cw[pl.ds(pl.multiple_of(row, 8), 16), :] = value[at : at + 16]
        return carry

    lax.fori_loop(0, 2, leaf_level, 0)

    def leaf_pack(r, carry):
        for k, first in ((0, 0), (1, 13)):
            for t in range(3):
                rows = [
                    cw[pl.ds(((r + u) * WI + 3 + first + t) * WJ + 8, 16), :] for u in (0, 4)
                ]
                crs[k, r, t] = sel(rows[0], rows[1]).astype(BF)
                cols = [
                    jnp.concatenate(
                        [
                            cw[
                                pl.ds(((r + u) * WI + 3 + 8 * v) * WJ + 8 + first + t, 8, stride=WJ),
                                :,
                            ]
                            for v in range(2)
                        ],
                        axis=0,
                    )
                    for u in (0, 4)
                ]
                ccs[k, r, t] = sel(cols[0], cols[1]).astype(BF)
        return carry

    for r in range(4):
        leaf_pack(r, 0)

    def leaf_box(i, j):
        return cw[pl.ds(i * WJ + j, 8, stride=WI * WJ), :]

    for (dx, dy), k in CORNERS.items():
        first_i, first_j = (3 if dx < 0 else 16), (8 if dy < 0 else 21)
        for t in range(3):
            box = [leaf_box(first_i + t, first_j + u) for u in range(3)]
            cks[k, t] = jnp.concatenate([sel(box[0], box[2]), box[1]], axis=0).astype(BF)
    for d in DIRS:
        start(leaf_copy(d), d)

    def twice(level):
        t = transfer_v[level]
        return jnp.concatenate([t, t], axis=1)

    def gather_one(i, carry):
        for j in range(0, 8, 2):
            tiles = []
            for u in range(2):
                box = [
                    leaf_box(3 + 2 * i + a, 8 + 2 * (j + u) + b) for a in range(2) for b in range(2)
                ]
                tiles.append(
                    jnp.concatenate([sel(box[0], box[1]), sel(box[2], box[3])], axis=1)
                )
            u1_v[pl.ds(i * 64 + j * 8, 16), :] = jnp.concatenate(tiles, axis=0).astype(BF)
        return carry

    for i in range(8):
        gather_one(i, 0)
    c1_v[...] = rounded(dot(u1_v[...], twice(0))).reshape(64, 8, 128)

    def quad_one(i, carry):
        for g in range(2):
            box = [c1_v[i * 8 + 4 * g + u] for u in range(4)]
            q1_v[3 + i, 1 + g] = jnp.concatenate(
                [sel(box[0], box[2]), sel(box[1], box[3])], axis=0
            ).astype(BF)
        return carry

    for i in range(8):
        quad_one(i, 0)
    for d in DIRS:
        start(one_copy(d), d)

    def parents(children, n, i, j):
        box = [children[(2 * i + a) * 2 * n + 2 * j + b] for a in range(2) for b in range(2)]
        return jnp.concatenate([sel(box[0], box[1]), sel(box[2], box[3])], axis=1)

    def quad(box):
        return jnp.concatenate([sel(box[0], box[2]), sel(box[1], box[3])], axis=0).astype(BF)

    for i in range(4):
        for j in range(0, 4, 2):
            u2_v[pl.ds((i * 4 + j) * 8, 16), :] = jnp.concatenate(
                [parents(c1_v, 4, i, j + u) for u in range(2)], axis=0
            ).astype(BF)
    c2_v[...] = rounded(dot(u2_v[...], twice(1))).reshape(16, 8, 128)
    for i in range(4):
        q2_v[3 + i, 1] = quad([c2_v[i * 4 + u] for u in range(4)])
    for d in DIRS:
        start(two_copy(d), d)
    up = jnp.concatenate(
        [parents(c2_v, 2, i, j) for i in range(2) for j in range(2)], axis=0
    ).astype(BF)
    c3 = rounded(dot(up, twice(2)))
    q3_v[3, 3] = quad([c3[u * 8 : (u + 1) * 8] for u in range(4)])
    for b in REACH:
        start(along_copy(b), (0, b))

    for c in list_loads:
        c.wait()
    lists_v[...] = jnp.full(lists_v.shape, -1000000.0, F32)
    lists_v[pl.ds(0, 256), pl.ds(0, 27)] = f0_v[...].astype(F32)
    lists_v[pl.ds(256, 64), pl.ds(0, 27)] = f1_v[...].astype(F32)
    for i in range(4):
        lists_v[pl.ds(320 + 4 * i, 4), pl.ds(0, 27)] = f2_v[i].astype(F32)
    for i in range(2):
        lists_v[pl.ds(336 + 2 * i, 2), pl.ds(0, 27)] = f3_v[i].astype(F32)
    lists_v[pl.ds(340, 1), pl.ds(0, 27)] = f4_v[0].astype(F32)
    nlist_v[...] = jnp.full(nlist_v.shape, -1000000.0, F32)
    for s in range(9):
        nlist_v[pl.ds(16 * s, 16), pl.ds(0, 16)] = nl_v[s].astype(F32)

    far_t = jnp.concatenate(
        [jnp.transpose(lists_v[pl.ds(128 * t, 128), :])[0:32] for t in range(3)], axis=1
    )
    lane = lax.broadcasted_iota(jnp.int32, (1, 384), 1)
    level_of = [(0, 0, 16, 4), (256, 1, 8, 3), (320, 2, 4, 2), (336, 3, 2, 1), (340, 4, 1, 0)]
    base = jnp.zeros((1, 384), jnp.int32)
    pitch = jnp.zeros((1, 384), jnp.int32)
    for first, level, n, shift in level_of:
        local = lane - first
        cols = n * size_y
        mine = (x * n + lax.shift_right_arithmetic(local, shift)) * cols + y * n + (local & (n - 1))
        base = jnp.where(local >= 0, mine, base)
        pitch = jnp.where(local >= 0, cols, pitch)
    far_t = far_t - base.astype(F32)
    pitch = pitch.astype(F32)
    counts_v[...] = jnp.zeros(counts_v.shape, F32)

    def far_count(p, carry):
        row = (p - 3).astype(F32) * pitch
        for k, q in enumerate((-3, -2, -1, 0, 1, None, 2, 3)):
            if q is not None:
                hits = jnp.where(far_t == row + float(q), 1.0, 0.0)
                counts_v[pl.ds(p * 8 + k, 1), :] = jnp.sum(hits, axis=0, keepdims=True)
        return carry

    lax.fori_loop(0, 7, far_count, 0)
    near_t = []
    group = lax.broadcasted_iota(jnp.int32, (16, 128), 1) // 16
    for half in range(2):
        got = jnp.full((16, 128), -1000000.0, F32)
        for k in range(8):
            piece = nlist_v[pl.ds(half * 8 + k, 16, stride=16), :]
            if k:
                piece = pltpu.roll(piece, 16 * k, 1)
            got = jnp.where(group == k, piece, got)
        near_t.append(got)
    near_t = jnp.concatenate(near_t, axis=1) - base[:, 0:256].astype(F32)
    for o, (p, q) in enumerate(NEAR):
        hits = jnp.where(near_t == float(p) * float(16 * size_y) + float(q), 1.0, 0.0)
        counts_v[pl.ds(64 + o, 1), pl.ds(0, 256)] = jnp.sum(hits, axis=0, keepdims=True)
    counts = jnp.concatenate(
        [jnp.transpose(counts_v[:, pl.ds(128 * t, 128)]) for t in range(3)], axis=0
    ).astype(BF)
    source = lax.broadcasted_iota(jnp.int32, (128, 256), 0)
    column = lax.broadcasted_iota(jnp.int32, (128, 256), 1)
    half_of = (column // 64) % 2
    second = column >= 128
    for t in range(0, PAIR_COUNT, 2):
        k = [(p + 3) * 8 + 2 * m for p, m in PAIRS[t : t + 2]]
        spread = jnp.where(source == jnp.where(second, k[1], k[0]) + half_of, 1.0, 0.0).astype(BF)
        weights = dot(counts, spread)
        w0_v[:, pl.ds(128 * t, 256)] = weights[0:256].astype(BF)
        w14_v[t] = weights[256:384, 0:128]
        w14_v[t + 1] = weights[256:384, 128:256]
    for o in range(0, 10, 2):
        spread = jnp.where(source == jnp.where(second, 65 + o, 64 + o), 1.0, 0.0).astype(BF)
        wn_v[:, pl.ds(128 * o, 256)] = dot(counts[0:256], spread).astype(BF)

    for d in DIRS:
        arrived(near_copy((-d[0], -d[1])), d)

    def near_unpack(r, carry):
        for k, ii, jj in ((0, 0, 7), (1, 17, 24)):
            for h in range(2):
                fw[h, pl.ds(pl.multiple_of((r * NI + ii) * WJ + 8, 8), 16), :] = nr[
                    k, r, :, pl.ds(h * 128, 128)
                ].astype(F32)
                column = nc[k, r, :, pl.ds(h * 128, 128)].astype(F32)
                for t in range(2):
                    fw[h, pl.ds((r * NI + 1 + 8 * t) * WJ + jj, 8, stride=WJ), :] = column[
                        8 * t : 8 * t + 8
                    ]
        return carry

    lax.fori_loop(0, NR_, near_unpack, 0)
    for (dx, dy), k in CORNERS.items():
        ii, jj = (0 if dx < 0 else 17), (7 if dy < 0 else 24)
        for h in range(2):
            fw[h, pl.ds(ii * WJ + jj, 8, stride=NI * WJ), :] = nk[k, :, pl.ds(h * 128, 128)]
    for c in weight_loads:
        c.wait()

    def near_rows(i):
        columns = []
        for o, (p, q) in enumerate(NEAR):
            w = wn_v[pl.ds(pl.multiple_of(i * 16, 16), 16), pl.ds(128 * o, 128)]
            for h in range(2):
                tiles = []
                for r in range(NR_):
                    first = (r * NI + i + 1 + p) * WJ + 8 + q
                    if q == 0:
                        first = pl.multiple_of(first, 8)
                    tiles.append(fw[h, pl.ds(first, 16), :].astype(BF) * w)
                columns.append(jnp.concatenate(tiles, axis=0))
        return jnp.concatenate(columns, axis=1)

    def near_block(block, carry):
        left = jnp.concatenate([near_rows(block * NEAR_ROWS + u) for u in range(NEAR_ROWS)], axis=0)
        rows = pl.ds(pl.multiple_of(block * (128 * NEAR_ROWS), 128 * NEAR_ROWS), 128 * NEAR_ROWS)
        acc_v[rows, :] = dot(left, near_v[...]).astype(BF)
        pltpu.make_async_copy(acc_v.at[rows], near_out_h.at[rows], out_sem.at[0]).start()
        return carry

    lax.fori_loop(0, 16 // NEAR_ROWS, near_block, 0)

    for b in REACH:
        arrived(along_copy(-b), (0, b))
    for a in REACH:
        start(across_copy(a), (a, 0))

    for d in DIRS:
        arrived(leaf_copy((-d[0], -d[1])), d)

    def leaf_unpack(r, carry):
        for k in range(2):
            for t in range(3):
                row = cr[k, r, t].astype(F32)
                other = swap(row)
                column = cc[k, r, t].astype(F32)
                across = swap(column)
                ii = t + (0, 19)[k]
                jj = t + (5, 24)[k]
                for u, value, col in (
                    (0, sel(row, other), sel(column, across)),
                    (4, sel(other, row), sel(across, column)),
                ):
                    cw[pl.ds(((r + u) * WI + ii) * WJ + 8, 16), :] = value
                    for v in range(2):
                        cw[pl.ds(((r + u) * WI + 3 + 8 * v) * WJ + jj, 8, stride=WJ), :] = col[
                            8 * v : 8 * v + 8
                        ]
        return carry

    for r in range(4):
        leaf_unpack(r, 0)
    for (dx, dy), k in CORNERS.items():
        for t in range(3):
            value = ck[k, t].astype(F32)
            other = swap(value)
            ii = t + (0 if dx < 0 else 19)
            for u in range(3):
                jj = u + (5 if dy < 0 else 24)
                rows = slice(8, 16) if u == 1 else slice(0, 8)
                box = sel(other, value) if u == 2 else sel(value, other)
                cw[pl.ds(ii * WJ + jj, 8, stride=WI * WJ), :] = box[rows]

    def pair_row(r, carry):
        for ii in range(WI):
            for m, q in enumerate(PAIR_Q):
                a = cw[pl.ds((r * WI + ii) * WJ + 8 + q, 16), :]
                b = cw[pl.ds((r * WI + ii) * WJ + 9 + q, 16), :]
                pairs_v[m, r * WI + ii] = sel(a, b).astype(BF)
        return carry

    lax.fori_loop(0, NR_, pair_row, 0)

    def leaf_rows(i):
        columns = []
        for t, (p, m) in enumerate(PAIRS):
            w = w0_v[pl.ds(pl.multiple_of(i * 16, 16), 16), pl.ds(128 * t, 128)]
            columns.append(
                jnp.concatenate(
                    [pairs_v[m, r * WI + i + 3 + p] * w for r in range(NR_)], axis=0
                )
            )
        return jnp.concatenate(columns, axis=1)

    def leaf_block(block, carry):
        left = jnp.concatenate([leaf_rows(block * LEAF_ROWS + u) for u in range(LEAF_ROWS)], axis=0)
        rows = pl.ds(pl.multiple_of(block * (128 * LEAF_ROWS), 128 * LEAF_ROWS), 128 * LEAF_ROWS)
        y0_v[rows, :] = dot(left, coupling_v[0])
        return carry

    lax.fori_loop(0, 16 // LEAF_ROWS, leaf_block, 0)

    for d in DIRS:
        arrived(one_copy((-d[0], -d[1])), d)
        arrived(two_copy((-d[0], -d[1])), d)
    for a in REACH:
        arrived(across_copy(-a), (a, 0))

    def quad_parts(value):
        value = value.astype(F32)
        low, high = value[0:8], value[8:16]
        return low, high, swap(low), swap(high)

    def quad_row(dst, row, quads, first, last):
        parts = [quad_parts(v) for v in quads]
        for g, (lo, hi, lo_s, hi_s) in enumerate(parts):
            values = [sel(lo, hi_s), sel(hi, lo), sel(lo_s, hi)]
            if g + 1 < len(parts):
                values.append(sel(hi_s, parts[g + 1][2]))
            for u, value in enumerate(values):
                col = 4 * g + u - 1
                if first <= col < last:
                    dst[row, col] = value

    def rows_one(i, carry):
        quad_row(d1_v, i, [q1_v[i, g] for g in range(4)], 0, 13)
        return carry

    for i in range(14):
        rows_one(i, 0)

    def rows_two(i, carry):
        quad_row(d2_v, i, [q2_v[i, g] for g in range(3)], 0, 9)
        return carry

    for i in range(10):
        rows_two(i, 0)

    for dev in range(7):
        parts = [quad_parts(q3_v[dev, g]) for g in range(7)]
        for a in range(2):
            if 3 <= 2 * dev + a <= 10:
                for col in range(7):
                    g, b = (col + 3) // 2, (col + 3) % 2
                    lo, hi, lo_s, hi_s = parts[g]
                    lo_n, _, lo_sn, _ = parts[g + 1]
                    if b == 0:
                        value = sel(lo, hi_s) if a == 0 else sel(lo_s, hi)
                    else:
                        value = sel(hi, lo_sn) if a == 0 else sel(hi_s, lo_n)
                    d3_v[2 * dev + a - 3, col] = value
        for g in range(7):
            lo, hi, lo_s, hi_s = parts[g]
            u4_v[dev, pl.ds(g * 8, 8), :] = jnp.concatenate([sel(lo, hi_s), sel(lo_s, hi)], axis=1)
    c4_v[...] = rounded(dot(u4_v[...].reshape(392, 256).astype(BF), twice(3))).reshape(7, 56, 128)
    for i in range(7):
        for j in range(6):
            d4_v[i, j] = sel(c4_v[i, pl.ds(8 * j, 8), :], c4_v[i, pl.ds(8 * j + 8, 8), :])

    def fill(dst, window, n, first):
        def two_boxes(h, carry):
            tiles = []
            places = []
            for u in range(2):
                b = h * 2 + u if n > 1 else 0
                places.append((b // n, b % n, first + b))
            for t, (p, m) in enumerate(PAIRS):
                tiles = []
                for i, j, b in places:
                    w = w14_v[t, pl.ds(b, 1), :]
                    tiles.append(window[i + 3 + p, j + 3 + PAIR_Q[m]] * jnp.broadcast_to(w, (8, 128)))
                dst[pl.ds(aligned(h * 16, 16), 16), pl.ds(128 * t, 128)] = jnp.concatenate(tiles, axis=0).astype(BF)
            return carry

        if n < 8:
            for h in range(max(1, n * n // 2)):
                two_boxes(h, 0)
        else:
            def eight_boxes(h, carry):
                for u in range(4):
                    two_boxes(4 * h + u, carry)
                return carry

            lax.fori_loop(0, n * n // 8, eight_boxes, 0)

    fill(x4_v, d4_v, 1, 84)
    fill(x3_v, d3_v, 2, 80)
    fill(x2_v, d2_v, 4, 64)
    fill(x1_v, d1_v, 8, 0)
    down = dot(x4_v[...], coupling_v[4])[0:8].astype(BF)
    for level, n, xs, ys in ((3, 2, x3_v, y3_v), (2, 4, x2_v, y2_v), (1, 8, x1_v, y1_v)):
        ys[...] = dot(xs[...], coupling_v[level])
        for a in range(2):
            for b in range(2):
                spread = dot_t(down, transfer_v[level, pl.ds((2 * a + b) * 64, 64), :])
                for i in range(n // 2):
                    for j in range(n // 2):
                        at = ((2 * i + a) * n + 2 * j + b) * 8
                        part = (i * (n // 2) + j) * 8
                        ys[pl.ds(at, 8), :] += spread[part : part + 8]
        down = ys[...].astype(BF)
    for a in range(2):
        for b in range(2):
            t = transfer_v[0, pl.ds((2 * a + b) * 64, 64), :]
            spread = dot_t(down, jnp.concatenate([t, t], axis=0))
            for i in range(8):
                for j in range(8):
                    at = (2 * i + a) * 128 + 2 * j + b
                    part = (i * 8 + j) * 8
                    g_v[pl.ds(at, 8, stride=16), :] = spread[part : part + 8]

    d0_v[...] = (y0_v[...] + g_v[:, pl.ds(0, 64)]).astype(BF)
    leaf_out = pltpu.make_async_copy(d0_v, leaf_out_h, out_sem.at[1])
    leaf_out.start()
    for d in DIRS:
        for copy in (near_copy, leaf_copy, one_copy, two_copy):
            sent(copy(d), d)
    for b in REACH:
        sent(along_copy(b), (0, b))
    for a in REACH:
        sent(across_copy(a), (a, 0))
    pltpu.make_async_copy(acc_v, near_out_h, out_sem.at[0]).wait()
    leaf_out.wait()


def finish(
    near_h, leaf_h, basis_h, amp_h, out_h, near_v, leaf_v, basis_v, amp_v, out_v, load_sem, out_sem
):
    small = [
        pltpu.make_async_copy(amp_h, amp_v, load_sem.at[0]),
        pltpu.make_async_copy(basis_h, basis_v, load_sem.at[1]),
    ]
    size = 2048 // PARTS
    parts = [pl.ds(n * size, size) for n in range(PARTS)]
    leaf = [
        pltpu.make_async_copy(leaf_h.at[p], leaf_v.at[p], load_sem.at[2 + n])
        for n, p in enumerate(parts)
    ]
    near = [
        pltpu.make_async_copy(near_h.at[p], near_v.at[p], load_sem.at[2 + PARTS + n])
        for n, p in enumerate(parts)
    ]
    outs = [
        pltpu.make_async_copy(out_v.at[p], out_h.at[p], out_sem.at[n]) for n, p in enumerate(parts)
    ]
    for n in range(PARTS):
        leaf[n].start()
        near[n].start()
        if n == 0:
            for c in small:
                c.start()
    for c in small:
        c.wait()
    for n, p in enumerate(parts):
        leaf[n].wait()
        far = dot(leaf_v[p, :], basis_v[...])
        near[n].wait()
        value = near_v[p, :].astype(F32) + far
        for i in range(size // 128):
            first = n * size + i * 128
            amp = amp_v[pl.ds(first // 8, 16), :]
            rows = value[i * 128 : (i + 1) * 128].reshape(NR_, 16, 256) * amp[None]
            for v in range(2):
                part = jnp.swapaxes(rows[:, 8 * v : 8 * v + 8], 0, 1)
                out_v[pl.ds(first + v * 64, 64), :] = part.reshape(64, 256)
        outs[n].start()
    for c in outs:
        c.wait()


def body(
    right_sides, amplitude, near_list, far_leaf, far_one, far_two, far_three, far_four,
    basis, transfer, coupling, near_tiles,
):
    size_x, size_y = lax.axis_size("bx"), lax.axis_size("by")
    dma = pltpu.SemaphoreType.DMA
    vmem = pltpu.VMEM
    i32 = jnp.int32
    operands = (
        right_sides.reshape(2048, 256), amplitude.reshape(256, 256),
        jnp.transpose(near_list, (2, 0, 1)), far_leaf.reshape(256, 27), far_one.reshape(64, 27),
        far_two, far_three, far_four, basis.T, transfer.reshape(4, 256, 64),
        coupling.reshape(5, 2560, 64), near_tiles.reshape(2304, 256),
    )
    scratch = [
        vmem((2, 2048, 128), F32), vmem((2, 256, 128), F32), vmem((9, 16, 16), i32),
        vmem((256, 27), i32), vmem((64, 27), i32), vmem((4, 4, 27), i32), vmem((2, 2, 27), i32),
        vmem((1, 1, 27), i32), vmem((64, 256), BF), vmem((4, 256, 64), BF),
        vmem((5, SLOTS * 64, 64), BF), vmem((2304, 256), BF),
        vmem((8, 16, 16, 256), BF), vmem((2, NR_ * NI * WJ, 128), F32),
        vmem((NR_ * WI * WJ, 128), F32), vmem((2048, 128), F32), vmem((4, NR_ * WI, 16, 128), BF),
        vmem((384, 128), F32), vmem((256, 128), F32), vmem((128, 384), F32),
        vmem((256, 10 * 128), BF), vmem((256, PAIR_COUNT * 128), BF), vmem((PAIR_COUNT, 128, 128), F32),
        vmem((2, 8, 16, 256), BF), vmem((4, 8, 256), F32),
        vmem((2, 8, 16, 256), BF), vmem((2, 8, 16, 256), BF), vmem((4, 8, 256), F32),
        vmem((2, 4, 3, 16, 128), BF), vmem((2, 4, 3, 16, 128), BF), vmem((4, 3, 16, 128), BF),
        vmem((2, 4, 3, 16, 128), BF), vmem((2, 4, 3, 16, 128), BF), vmem((4, 3, 16, 128), BF),
        vmem((512, 256), BF), vmem((64, 8, 128), F32), vmem((128, 256), BF), vmem((16, 8, 128), F32),
        vmem((14, 4, 16, 128), BF), vmem((10, 3, 16, 128), BF), vmem((7, 7, 16, 128), BF),
        vmem((7, 56, 256), F32), vmem((7, 56, 128), F32),
        vmem((14, 13, 8, 128), F32), vmem((10, 9, 8, 128), F32), vmem((8, 7, 8, 128), F32),
        vmem((7, 6, 8, 128), F32),
        vmem((512, SLOTS * 64), BF), vmem((128, SLOTS * 64), BF), vmem((32, SLOTS * 64), BF),
        vmem((16, SLOTS * 64), BF),
        vmem((512, 64), F32), vmem((128, 64), F32), vmem((32, 64), F32), vmem((16, 64), F32),
        vmem((2048, 256), BF), vmem((2048, 64), F32), vmem((2048, 64), BF),
        dma((12,)), dma((6,)), dma((6,)), dma((2,)),
        dma((8,)), dma((8,)), dma((8,)), dma((8,)), dma((8,)), dma((8,)), dma((8,)), dma((8,)),
        dma((12,)), dma((12,)),
    ]
    near, leaf = pl.pallas_call(
        functools.partial(kernel, size_x, size_y),
        out_shape=[jax.ShapeDtypeStruct((2048, 256), BF), jax.ShapeDtypeStruct((2048, 64), BF)],
        in_specs=[pl.BlockSpec(memory_space=pl.ANY)] * len(operands),
        out_specs=[pl.BlockSpec(memory_space=pl.ANY)] * 2,
        scratch_shapes=scratch,
        compiler_params=pltpu.CompilerParams(
            collective_id=0, has_side_effects=True, vmem_limit_bytes=56 * 1024 * 1024
        ),
        cost_estimate=pl.CostEstimate(
            flops=12_000_000_000, bytes_accessed=10_000_000, transcendentals=0
        ),
    )(*operands)
    product = pl.pallas_call(
        finish,
        out_shape=jax.ShapeDtypeStruct((2048, 256), F32),
        in_specs=[pl.BlockSpec(memory_space=pl.ANY)] * 4,
        out_specs=pl.BlockSpec(memory_space=pl.ANY),
        scratch_shapes=[
            vmem((2048, 256), BF), vmem((2048, 64), BF), vmem((64, 256), BF), vmem((256, 256), F32),
            vmem((2048, 256), F32), dma((2 + 2 * PARTS,)), dma((PARTS,)),
        ],
        compiler_params=pltpu.CompilerParams(vmem_limit_bytes=60 * 1024 * 1024),
        cost_estimate=pl.CostEstimate(
            flops=100_000_000, bytes_accessed=4_000_000, transcendentals=0
        ),
    )(near, leaf, operands[8], operands[1])
    return product.reshape(right_sides.shape)


def solution(mesh):
    split3 = P("bx", "by", None)
    placed = (P("bx", "by", None, None),) + (split3,) * 7 + (P(),) * 4
    return jax.shard_map(
        body, mesh=mesh, in_specs=placed, out_specs=P("bx", "by", None, None), check_vma=False
    )
```
